32 devices in a mesh: group: 2 (over x), expert: 16 (over z, y, core).
Axes of the slice: x: 2, y: 2, z: 4, core: 2. Of those that a mesh axis runs over, the one named last changes fastest.
Arguments:
- resid: bfloat16 [4096, 2048], P(('group', 'expert')), may hold values from -6 to 6
- queries: bfloat16 [4096, 2048], P(('group', 'expert')), may hold values from -48 to 48
- span_kv: bfloat16 [2, 4096, 2048], P(None, ('group', 'expert')), may hold values from -4 to 4
- cache_kv: bfloat16 [2, 32, 2, 128, 2048], P(None, ('group', 'expert')), may hold values from -6 to 6
- seg_len: int32 [32, 2], P(('group', 'expert')), may hold values from 0 to 128, as said below
- o_rows: bfloat16 [2048, 2048], P('expert'), may hold values from -0.125 to 0.125
- norm_gain: float32 [2048], replicated, may hold values from 0.25 to 1.75
- routes: int32 [4096, 8], P(('group', 'expert')), may hold values from 0 to 15, all different within a row; in each aligned block of 128 rows (0 to 127, 128 to 255, ...) at most 96 rows name the same one
- route_wts: float32 [4096, 8], P(('group', 'expert')), may hold values from 0.05 to 0.6
- w_in: bfloat16 [16, 2048, 1024], P('expert'), may hold values from -0.125 to 0.125
- w_out: bfloat16 [16, 512, 2048], P('expert'), may hold values from -0.25 to 0.25
Outputs:
- layer_out: bfloat16 [4096, 2048], P(('group', 'expert'))
The draws below stay inside these ranges and needn't reach their ends.
Inputs may be any that keep to these rules, and one draw needn't show every extreme that they name: seg_len[d, 0] is 1 to 128; seg_len[d, 1] is 0 (the paired request is short) or 1 to 128; seg_len[0, 0] and seg_len[0, 1] are 128 and seg_len[1, 1] is 0. `routes`: each row names 8 different experts; among the 128 rows of one device no expert is named more than 96 times.
All inputs are finite; a program needn't handle non-finite values.
Results may differ from the reference program's by a relative error of at most 0.0053.
Values may be sent and summed in bfloat16 or wider, within the bound.
No kernel may reach another device: no remote copies, remote signals or barrier semaphores. Data moves between devices by JAX's collectives and lax.ppermute only.
A program may use at most 128 MiB of HBM per device.

```python
import math
import jax
import jax.numpy as jnp
import numpy as np
from jax import lax

HEADS = 16
HD = 128
D = 2048
FF = 512
TOPK = 8
SPAN = 128
SEG = 128
EXPERTS = 16
CAP = 96
DEVS = 32
TOKENS = 4096
N_GROUP = 2
N_EXPERT = 16


def joint_rows(key):
    key_q, key_k, key_v = jax.random.split(jax.random.fold_in(key, 7), 3)
    keys_raw = jnp.clip(jax.random.normal(key_k, (TOKENS, D), jnp.float32), -4.0, 4.0)
    queries_raw = jnp.clip(jax.random.normal(key_q, (TOKENS, D), jnp.float32), -4.0, 4.0)
    values_raw = jnp.clip(jax.random.normal(key_v, (TOKENS, D), jnp.float32), -4.0, 4.0)
    return (queries_raw, keys_raw, values_raw)


def draw_queries(key, part):
    queries_raw, keys_raw, values_raw = joint_rows(key)
    return queries_raw.astype(jnp.bfloat16)


def draw_span_kv(key, part):
    queries_raw, keys_raw, values_raw = joint_rows(key)
    return jnp.stack([keys_raw, values_raw]).astype(jnp.bfloat16)


def draw_seg_len(key, part):
    key_own, key_long, key_part = jax.random.split(jax.random.fold_in(key, 11), 3)
    own_length = jax.random.randint(key_own, (DEVS,), 1, SEG + 1).astype(jnp.int32)
    own_length = own_length.at[0].set(SEG)
    is_long = jax.random.randint(key_long, (DEVS,), 0, 2).astype(jnp.int32)
    long_length = jax.random.randint(key_part, (DEVS,), 1, SEG + 1).astype(jnp.int32)
    second = jnp.where(is_long == 1, long_length, 0)
    second = second.at[0].set(SEG).at[1].set(0)
    return jnp.stack([own_length, second], axis=1).astype(jnp.int32)


def block_levels(own_key, shape, pieces, low, high):
    factor_of, own = 1.0, jax.random.fold_in(own_key, 6)
    for axis_at, parts in pieces:
        draws = jnp.exp(jax.random.uniform(jax.random.fold_in(own, axis_at), (parts,), jnp.float32, low / len(pieces), high / len(pieces)))
        factor_of = factor_of * jnp.repeat(draws, shape[axis_at] // parts).reshape([-1 if axis == axis_at else 1 for axis in range(len(shape))])
    return factor_of


def assign_block(own_key, own, number, rows, number_of, top, most, skew):
    sequence = jax.random.permutation(own_key, number_of)
    crowded, usual = load_shares(number_of, rows * top, most, skew, True), load_shares(number_of, rows * top, most, skew, False)
    places = jnp.arange(number_of)

    def named(lengths, offset_by):
        used = int((lengths > 0).sum())
        fixed = max(1, used // 4)
        passed = fixed + (places - fixed + offset_by * (used - fixed)) % max(1, number_of - fixed)
        return jnp.zeros((number_of,), jnp.int32).at[sequence[jnp.where(places < fixed, places, passed)]].set(jnp.asarray(lengths, jnp.int32))

    lengths = jnp.where(number % 4 == 0, named(crowded, number // 4), named(usual, number - number // 4 - 1))
    mixed = jax.random.permutation(jax.random.fold_in(own, 3), number_of)
    donor, receiver = mixed[0:number_of // 2 * 2:2], mixed[1:number_of // 2 * 2:2]
    room = jnp.minimum(lengths[donor] - 1, most - lengths[receiver]) // 2
    room = jnp.where((donor == sequence[0]) | (receiver == sequence[0]) | (lengths[receiver] == 0), 0, jnp.maximum(room, 0))
    passed = jax.random.randint(jax.random.fold_in(own, 4), (number_of // 2,), 0, 1 << 20) % (room + 1)
    lengths = lengths.at[donor].add(-passed).at[receiver].add(passed)
    members = jnp.searchsorted(jnp.cumsum(lengths), jnp.arange(rows * top), side="right").astype(jnp.int32)
    grid = members.reshape(top, rows).T
    grid = grid[jax.random.permutation(jax.random.fold_in(own, 1), rows)]
    offset_by = jax.random.randint(jax.random.fold_in(own, 2), (rows, 1), 0, top)
    return jnp.take_along_axis(grid, (jnp.arange(top)[None, :] + offset_by) % top, axis=1)


def load_shares(amount, total, bound, skew, full):
    loads = [(1 << 20) // math.isqrt(grade ** skew) + 1 for grade in range(1, amount + 1)]
    largest = bound if full else min(bound, max(-(-total // amount), total * loads[0] // sum(loads)))
    least = 1 if total - largest >= amount - 1 else 0
    holding, rest = [largest] + [least] * (amount - 1), total - largest - least * (amount - 1)
    while rest > 0:
        movable = [i for i in range(1, amount) if holding[i] < largest] or [i for i in range(1, amount) if holding[i] < bound]
        pool, budget = sum([loads[i] for i in movable]), rest
        for i in movable:
            addition = min(bound - holding[i], max(1, budget * loads[i] // pool), rest)
            holding[i] = holding[i] + addition
            rest = rest - addition
    return np.array(holding)


def scatter_about(own_key, extent, scale, limit, pieces=(), held_as=jnp.bfloat16):
    result = scale * jax.random.normal(own_key, extent, jnp.float32)
    if pieces:
        result = result * block_levels(own_key, extent, pieces, -0.22, 0.18)
    return jnp.clip(result, -limit, limit).astype(held_as)


def setup_inputs(seed: int = 0) -> dict:
    streams_of = jax.random.split(jax.random.key(seed), 12)
    resid = scatter_about(streams_of[0], (TOKENS, D), 1.0, 6.0, ((0, 32),))
    queries = draw_queries(jax.random.fold_in(streams_of[11], 71), 0)
    span_kv = draw_span_kv(jax.random.fold_in(streams_of[11], 71), 0)
    cache_kv = scatter_about(streams_of[3], (2, DEVS, 2, SEG, D), 1.0, 6.0, ((1, 32),))
    seg_len = draw_seg_len(jax.random.fold_in(streams_of[11], 71), 0)
    o_rows = scatter_about(streams_of[5], (D, D), D ** -0.5, 0.125, ((0, 16),))
    norm_gain = jnp.clip(1.0 + 0.15 * jax.random.normal(streams_of[6], (D,), jnp.float32), 0.25, 1.75)
    routes_keys = jax.random.split(jax.random.fold_in(streams_of[7], 1), TOKENS // SPAN)
    routes_turns = jax.random.permutation(jax.random.fold_in(streams_of[7], 3), TOKENS // SPAN)
    routes = jax.vmap(lambda own, number: assign_block(jax.random.fold_in(streams_of[7], 2), own, number, SPAN, EXPERTS, TOPK, CAP, 1))(routes_keys, routes_turns).reshape((TOKENS, TOPK))
    route_wts = jnp.clip(0.05 + 0.55 * jax.random.uniform(streams_of[8], (TOKENS, TOPK), jnp.float32) ** block_levels(streams_of[8], (TOKENS, TOPK), ((0, 32),), -0.2, 0.2), 0.05, 0.6)
    w_in = scatter_about(streams_of[9], (EXPERTS, D, 2 * FF), D ** -0.5, 0.125, ((0, 16),))
    w_out = scatter_about(streams_of[10], (EXPERTS, FF, D), FF ** -0.5, 0.25, ((0, 16),))
    return dict(resid=resid, queries=queries, span_kv=span_kv, cache_kv=cache_kv, seg_len=seg_len, o_rows=o_rows, norm_gain=norm_gain, routes=routes, route_wts=route_wts, w_in=w_in, w_out=w_out)


def attend(query_rows, key_rows, value_rows, valid_keys):
    q_heads = query_rows.astype(jnp.float32).reshape(-1, HEADS, HD)
    k_heads = key_rows.astype(jnp.float32).reshape(-1, HEADS, HD)
    v_heads = value_rows.astype(jnp.float32).reshape(-1, HEADS, HD)
    scores = jnp.einsum('chd,shd->hcs', q_heads, k_heads) * (1.0 / math.sqrt(HD))
    scores = jnp.where(valid_keys[None, None, :], scores, -1e+30)
    peak_score = lax.optimization_barrier(jnp.max(scores, axis=-1))
    expo = jnp.where(valid_keys[None, None, :], jnp.exp(scores - peak_score[..., None]), 0.0)
    totals = lax.optimization_barrier(jnp.sum(expo, axis=-1))
    probs_low = expo.astype(jnp.bfloat16).astype(jnp.float32)
    accum_out = jnp.einsum('hcs,shd->chd', probs_low, v_heads)
    return (peak_score, totals, accum_out)

def merge_parts(first, second):
    peak_a, total_a, accum_a = first
    peak_b, total_b, accum_b = second
    peak_both = jnp.maximum(peak_a, peak_b)
    scale_a = jnp.exp(peak_a - peak_both).T
    scale_b = jnp.exp(peak_b - peak_both).T
    numer = accum_a * scale_a[:, :, None] + accum_b * scale_b[:, :, None]
    denom = total_a.T * scale_a + total_b.T * scale_b
    merged = numer / denom[:, :, None]
    return merged.reshape(merged.shape[0], -1).astype(jnp.bfloat16)

def slot_of(route_rows):
    onehot = (route_rows[:, :, None] == jnp.arange(EXPERTS, dtype=jnp.int32)[None, None, :]).astype(jnp.int32)
    counts = lax.optimization_barrier(jnp.sum(onehot, axis=1))
    before = jnp.cumsum(counts, axis=0) - counts
    return lax.optimization_barrier(jnp.sum(onehot * before[:, None, :], axis=-1))

def expert_mlp(token_rows, weight_in, weight_out):
    joined = jnp.dot(token_rows, weight_in, preferred_element_type=jnp.float32)
    hidden = (jax.nn.silu(joined[:, :FF]) * joined[:, FF:]).astype(jnp.bfloat16)
    return jnp.dot(hidden, weight_out, preferred_element_type=jnp.float32).astype(jnp.bfloat16)

def reference(resid, queries, span_kv, cache_kv, seg_len, o_rows, norm_gain, routes, route_wts, w_in, w_out):
    query_blocks = queries.reshape(DEVS, SPAN, D)
    span_keys = span_kv[0].reshape(DEVS, SPAN, D)
    span_vals = span_kv[1].reshape(DEVS, SPAN, D)
    positions = jnp.arange(SEG, dtype=jnp.int32)

    def one_request(device):
        partner = jnp.bitwise_xor(device // N_EXPERT, 1) * N_EXPERT + device % N_EXPERT
        keys_a = jnp.concatenate([span_keys[device], cache_kv[0, device, 0]], axis=0)
        vals_a = jnp.concatenate([span_vals[device], cache_kv[1, device, 0]], axis=0)
        valid_a = jnp.concatenate([jnp.ones((SPAN,), bool), positions < seg_len[device, 0]])
        part_a = attend(query_blocks[device], keys_a, vals_a, valid_a)
        valid_b = positions < seg_len[partner, 1]
        part_b = attend(query_blocks[device], cache_kv[0, partner, 1], cache_kv[1, partner, 1], valid_b)
        return merge_parts(part_a, part_b)
    attended = lax.map(one_request, jnp.arange(DEVS, dtype=jnp.int32)).reshape(TOKENS, D)
    residual = resid.astype(jnp.float32) + jnp.dot(attended, o_rows, preferred_element_type=jnp.float32)
    normed = (residual * lax.rsqrt(lax.optimization_barrier(jnp.mean(residual * residual, axis=-1, keepdims=True)) + 1e-05) * norm_gain).astype(jnp.bfloat16)

    def one_group(group_id):
        start_row = (group_id * (N_EXPERT * SPAN)).astype(jnp.int32)
        group_acts = lax.dynamic_slice_in_dim(normed, start_row, N_EXPERT * SPAN, 0)
        group_resid = lax.dynamic_slice_in_dim(residual, start_row, N_EXPERT * SPAN, 0).reshape(N_EXPERT, SPAN, D)
        group_routes = lax.dynamic_slice_in_dim(routes, start_row, N_EXPERT * SPAN, 0).reshape(N_EXPERT, SPAN, TOPK)
        group_weights = lax.dynamic_slice_in_dim(route_wts, start_row, N_EXPERT * SPAN, 0).reshape(N_EXPERT, SPAN, TOPK)
        slot_ids = jax.vmap(slot_of)(group_routes)
        source = jnp.arange(N_EXPERT, dtype=jnp.int32)[:, None, None]
        buffer_pos = (group_routes * N_EXPERT + source) * CAP + slot_ids
        token_ids = jnp.broadcast_to(source * SPAN + jnp.arange(SPAN, dtype=jnp.int32)[None, :, None], buffer_pos.shape)
        slot_token = jnp.full((EXPERTS * N_EXPERT * CAP,), -1, jnp.int32).at[buffer_pos.reshape(-1)].set(token_ids.reshape(-1))
        token_rows = jnp.where((slot_token >= 0)[:, None], group_acts[jnp.maximum(slot_token, 0)], jnp.zeros((), jnp.bfloat16))
        token_rows = token_rows.reshape(EXPERTS, N_EXPERT * CAP, D)
        outputs = lax.map(lambda items: expert_mlp(items[0], items[1], items[2]), (token_rows, w_in, w_out))
        outputs = outputs.reshape(EXPERTS * N_EXPERT * CAP, D)
        expert_sum = jnp.zeros((N_EXPERT, SPAN, D), jnp.float32)
        for route_k in range(TOPK):
            picked = outputs[buffer_pos[:, :, route_k]].astype(jnp.float32)
            expert_sum = expert_sum + group_weights[:, :, route_k, None] * picked
        return (group_resid + expert_sum).astype(jnp.bfloat16).reshape(N_EXPERT * SPAN, D)
    layer_out = lax.map(one_group, jnp.arange(N_GROUP, dtype=jnp.int32))
    return layer_out.reshape(TOKENS, D)
```

```python
import functools
import math

import jax
import jax.numpy as jnp
from jax import lax
from jax.experimental import pallas as pl
from jax.experimental.pallas import tpu as pltpu
from jax.sharding import PartitionSpec as P

HEADS = 16
HD = 128
FF = 512
F32 = jnp.float32
BF16 = jnp.bfloat16
SMEM = pltpu.SMEM


class Ring:
    def __init__(self, count):
        self.count = count
        self.pairs = count // 2
        chips = list(range(0, self.pairs, 2)) + list(range(1, self.pairs, 2))[::-1]
        self.device = [[2 * c, 2 * c + 1] for c in chips]
        self.place = {self.device[i][k]: (i, k) for i in range(self.pairs) for k in (0, 1)}

    def at(self, i, k):
        return self.device[i % self.pairs][k]

    def step(self):
        route = []
        for i in range(self.pairs):
            route += [(self.at(i, 0), self.at(i + 1, 0)), (self.at(i, 1), self.at(i - 1, 1))]
        return route

    def sibling(self):
        return [(e, e ^ 1) for e in range(self.count)]

    def source(self, s, flip_lane, flip_way):
        out = []
        for e in range(self.count):
            i, k = self.place[e]
            way = 1 if k == 0 else -1
            if flip_way:
                way = -way
            out.append(self.at(i - s * way, k ^ flip_lane))
        return out


def swap_pairs(axis):
    count = lax.axis_size(axis)
    route = []
    for low in range(0, count - 1, 2):
        route += [(low, low + 1), (low + 1, low)]
    return route


def attend_body(len_ref, far_len_ref, q_ref, kv_ref, near_ref, fk_ref, fv_ref, out_ref):
    rows = q_ref.shape[0]
    seg = fk_ref.shape[0]
    near_len = len_ref[0, 0]
    far_len = far_len_ref[0]
    pos = lax.broadcasted_iota(jnp.int32, (rows, seg), 1)
    near_ok = pos < near_len
    far_ok = pos < far_len
    scale = 1.0 / math.sqrt(HD)
    dims = (((1,), (1,)), ((), ()))
    for h in range(q_ref.shape[1] // HD):
        cols = slice(h * HD, (h + 1) * HD)
        q = q_ref[:, cols]
        s0 = lax.dot_general(q, kv_ref[0, :, cols], dims, preferred_element_type=F32) * scale
        s1 = lax.dot_general(q, near_ref[0, 0, 0, :, cols], dims, preferred_element_type=F32) * scale
        s2 = lax.dot_general(q, fk_ref[:, cols], dims, preferred_element_type=F32) * scale
        s1 = jnp.where(near_ok, s1, -1e30)
        s2 = jnp.where(far_ok, s2, -1e30)
        m = jnp.maximum(
            jnp.max(s0, axis=1, keepdims=True),
            jnp.max(jnp.maximum(s1, s2), axis=1, keepdims=True),
        )
        w0 = jnp.exp(s0 - m)
        w1 = jnp.where(near_ok, jnp.exp(s1 - m), 0.0)
        w2 = jnp.where(far_ok, jnp.exp(s2 - m), 0.0)
        l = jnp.sum(w0, axis=1, keepdims=True) + jnp.sum(w1 + w2, axis=1, keepdims=True)
        a = jnp.dot(w0.astype(BF16), kv_ref[1, :, cols], preferred_element_type=F32)
        a += jnp.dot(w1.astype(BF16), near_ref[1, 0, 0, :, cols], preferred_element_type=F32)
        a += jnp.dot(w2.astype(BF16), fv_ref[:, cols], preferred_element_type=F32)
        out_ref[h] = (a / l).astype(BF16)


def attend(queries, span_kv, cache_kv, far_k, far_v, seg_len, far_len):
    rows, width = queries.shape
    seg = far_k.shape[0]
    per = 4
    wide = per * HD
    return pl.pallas_call(
        attend_body,
        grid=(width // wide,),
        out_shape=jax.ShapeDtypeStruct((width // HD, rows, HD), BF16),
        in_specs=[
            pl.BlockSpec(memory_space=SMEM),
            pl.BlockSpec(memory_space=SMEM),
            pl.BlockSpec((rows, wide), lambda i: (0, i)),
            pl.BlockSpec((2, rows, wide), lambda i: (0, 0, i)),
            pl.BlockSpec((2, 1, 1, seg, wide), lambda i: (0, 0, 0, 0, i)),
            pl.BlockSpec((seg, wide), lambda i: (0, i)),
            pl.BlockSpec((seg, wide), lambda i: (0, i)),
        ],
        out_specs=pl.BlockSpec((per, rows, HD), lambda i: (i, 0, 0)),
        cost_estimate=pl.CostEstimate(
            flops=12 * rows * rows * width, bytes_accessed=16 * rows * width, transcendentals=0
        ),
        compiler_params=pltpu.CompilerParams(vmem_limit_bytes=16 * 2**20),
        name="attend",
    )(seg_len, far_len, queries, span_kv, cache_kv, far_k, far_v)


def project_body(count, idx_ref, mine_ref, theirs_ref, *refs):
    blocks, (own_ref, give_ref) = refs[:count], refs[count:]
    rows = mine_ref.shape[1]
    total = None
    for b in range(count):
        i = idx_ref[b]
        both = jnp.concatenate([mine_ref[i], theirs_ref[i]], axis=0)
        part = jnp.dot(both, blocks[b][...], preferred_element_type=F32)
        total = part if total is None else total + part
    own_ref[...] = total[:rows]
    give_ref[...] = total[rows:]


def project(index, mine, theirs, blocks):
    count = len(blocks)
    rows = mine.shape[1]
    half = blocks[0].shape[1]
    full = pl.BlockSpec(memory_space=pltpu.VMEM)
    out = jax.ShapeDtypeStruct((rows, half), F32)
    return pl.pallas_call(
        functools.partial(project_body, count),
        out_shape=(out, out),
        in_specs=[pl.BlockSpec(memory_space=SMEM)] + [full] * (2 + count),
        out_specs=(full, full),
        cost_estimate=pl.CostEstimate(
            flops=8 * rows * half * half * 2, bytes_accessed=4 * half * half, transcendentals=0
        ),
        compiler_params=pltpu.CompilerParams(vmem_limit_bytes=24 * 2**20),
        name="project",
    )(index, mine, theirs, *blocks)


def norm_body(lane_ref, resid_ref, own_ref, got_ref, gain_ref, sum_ref, out_ref):
    first = lane_ref[0] == 0
    half = own_ref.shape[1]
    own = own_ref[...]
    got = got_ref[...]
    low = resid_ref[:, :half].astype(F32) + jnp.where(first, own, got)
    high = resid_ref[:, half:].astype(F32) + jnp.where(first, got, own)
    sum_ref[:, :half] = low
    sum_ref[:, half:] = high
    square = jnp.sum(low * low + high * high, axis=1, keepdims=True)
    scale = lax.rsqrt(square * (1.0 / (2 * half)) + 1e-05)
    out_ref[:, :half] = (low * scale * gain_ref[:, :half]).astype(BF16)
    out_ref[:, half:] = (high * scale * gain_ref[:, half:]).astype(BF16)


def norm(lane, resid, own, got, gain):
    full = pl.BlockSpec(memory_space=pltpu.VMEM)
    return pl.pallas_call(
        norm_body,
        out_shape=(
            jax.ShapeDtypeStruct(resid.shape, F32),
            jax.ShapeDtypeStruct(resid.shape, BF16),
        ),
        in_specs=[pl.BlockSpec(memory_space=SMEM)] + [full] * 4,
        out_specs=(full, full),
        cost_estimate=pl.CostEstimate(
            flops=8 * resid.size, bytes_accessed=12 * resid.size, transcendentals=0
        ),
        compiler_params=pltpu.CompilerParams(vmem_limit_bytes=16 * 2**20),
        name="norm",
    )(lane, resid, own, got, gain.reshape(1, -1))


def expert_body(src_ref, x_ref, y_ref, wt_ref, gate_ref, up_ref, down_ref, cx_ref, cy_ref, acc_ref):
    j = pl.program_id(0)
    rows = x_ref.shape[0]
    both = jnp.concatenate([x_ref[...], y_ref[...]], axis=0)
    gate = jnp.dot(both, gate_ref[0], preferred_element_type=F32)
    up = jnp.dot(both, up_ref[0], preferred_element_type=F32)
    hidden = (gate * jax.nn.sigmoid(gate) * up).astype(BF16)
    part = jnp.dot(hidden, down_ref[0], preferred_element_type=F32)

    @pl.when(j == 0)
    def _():
        acc_ref[...] = part

    @pl.when(j > 0)
    def _():
        acc_ref[...] += part

    @pl.when(j == pl.num_programs(0) - 1)
    def _():
        lanes = lax.broadcasted_iota(jnp.int32, wt_ref.shape, 1)
        wts = wt_ref[...]
        wx = jnp.sum(jnp.where(lanes == src_ref[0], wts, 0.0), axis=1, keepdims=True)
        wy = jnp.sum(jnp.where(lanes == src_ref[1], wts, 0.0), axis=1, keepdims=True)
        cx_ref[...] = (acc_ref[:rows] * wx).astype(BF16)
        cy_ref[...] = (acc_ref[rows:] * wy).astype(BF16)


def expert(src, x, y, wts, w_in, w_out):
    rows, width = x.shape
    chunk = 256
    steps = FF // chunk
    whole = pl.BlockSpec((rows, width), lambda j: (0, 0))
    out = jax.ShapeDtypeStruct((rows, width), BF16)
    return pl.pallas_call(
        expert_body,
        grid=(steps,),
        out_shape=(out, out),
        in_specs=[
            pl.BlockSpec(memory_space=SMEM),
            whole,
            whole,
            pl.BlockSpec(wts.shape, lambda j: (0, 0)),
            pl.BlockSpec((1, width, chunk), lambda j: (0, 0, j)),
            pl.BlockSpec((1, width, chunk), lambda j: (0, 0, j + steps)),
            pl.BlockSpec((1, chunk, width), lambda j: (0, j, 0)),
        ],
        out_specs=(whole, whole),
        scratch_shapes=[pltpu.VMEM((2 * rows, width), F32)],
        cost_estimate=pl.CostEstimate(
            flops=12 * rows * width * FF, bytes_accessed=6 * width * FF, transcendentals=0
        ),
        compiler_params=pltpu.CompilerParams(vmem_limit_bytes=24 * 2**20),
        name="expert",
    )(src, x, y, wts, w_in, w_in, w_out)


def shards(
    ring, resid, queries, span_kv, cache_kv, seg_len, o_rows, norm_gain, routes, route_wts, w_in, w_out
):
    count, pairs = ring.count, ring.pairs
    rows, width = queries.shape
    half = width // 2
    me = lax.axis_index("expert")
    lane = me % 2
    forward, sibling = ring.step(), ring.sibling()

    def look(table):
        return jnp.asarray(table, jnp.int32)[me]

    def ahead(block):
        return lax.ppermute(block, "expert", forward)

    def across(block):
        return lax.ppermute(block, "expert", sibling)

    group_swap = swap_pairs("group")
    far_len = lax.ppermute(seg_len[0, 1:2], "group", group_swap)
    far_k = lax.ppermute(cache_kv[0, 0, 1], "group", group_swap)
    far_v = lax.ppermute(cache_kv[1, 0, 1], "group", group_swap)

    picks = routes[:, :, None] == jnp.arange(count, dtype=jnp.int32)[None, None, :]
    dense = jnp.sum(jnp.where(picks, route_wts[:, :, None], 0.0), axis=1)
    wts = lax.all_to_all(dense.T, "expert", split_axis=0, concat_axis=0, tiled=True).T

    own_half = lax.dynamic_slice_in_dim(o_rows, lane * half, half, 1)
    other_half = lax.dynamic_slice_in_dim(o_rows, (1 - lane) * half, half, 1)
    chain_a, chain_b = own_half, across(other_half)
    blocks, index = [chain_a, chain_b], [me, me ^ 1]
    for s in range(1, pairs):
        chain_a = ahead(chain_a)
        chain_b = ahead(chain_b)
        blocks += [chain_a, chain_b]
        index += [look(ring.source(s, 0, False)), look(ring.source(s, 1, False))]

    mine = attend(queries, span_kv, cache_kv, far_k, far_v, seg_len, far_len)
    slab = o_rows.shape[0]
    if slab != HD:
        mine = mine.transpose(1, 0, 2).reshape(rows, count, slab).transpose(1, 0, 2)
    theirs = across(mine)
    own, give = project(jnp.stack(index), mine, theirs, blocks)
    got = across(give)
    residual, normed = norm(lane[None], resid, own, got, norm_gain)

    x = normed
    y = across(x)
    keep, give = expert(jnp.stack([me, me ^ 1]), x, y, wts, w_in, w_out)
    total = residual + keep.astype(F32) + across(give).astype(F32)
    travelling = None
    for s in range(1, pairs):
        x = ahead(x)
        y = across(x)
        src = jnp.stack([look(ring.source(s, 0, False)), look(ring.source(s, 1, True))])
        keep, give = expert(src, x, y, wts, w_in, w_out)
        part = keep.astype(F32) + across(give).astype(F32)
        if travelling is not None:
            part = part + travelling.astype(F32)
        travelling = ahead(part.astype(BF16))
    return (total + travelling.astype(F32)).astype(BF16)


def solution(mesh):
    placed = (
        P(("group", "expert"), None),
        P(("group", "expert"), None),
        P(None, ("group", "expert"), None),
        P(None, ("group", "expert"), None, None, None),
        P(("group", "expert"), None),
        P("expert", None),
        P(),
        P(("group", "expert"), None),
        P(("group", "expert"), None),
        P("expert", None, None),
        P("expert", None, None),
    )
    ring = Ring(mesh.shape["expert"])
    return jax.shard_map(
        functools.partial(shards, ring),
        mesh=mesh,
        in_specs=placed,
        out_specs=P(("group", "expert"), None),
        check_vma=False,
    )
```

```python
import functools
import math

import jax
import jax.numpy as jnp
from jax import lax
from jax.experimental import pallas as pl
from jax.experimental.pallas import tpu as pltpu
from jax.sharding import PartitionSpec as P

HEADS = 16
HD = 128
FF = 512
F32 = jnp.float32
BF16 = jnp.bfloat16
SMEM = pltpu.SMEM


class Ring:
    def __init__(self, count):
        self.count = count
        self.pairs = count // 2
        chips = list(range(0, self.pairs, 2)) + list(range(1, self.pairs, 2))[::-1]
        self.device = [[2 * c, 2 * c + 1] for c in chips]
        self.place = {self.device[i][k]: (i, k) for i in range(self.pairs) for k in (0, 1)}

    def at(self, i, k):
        return self.device[i % self.pairs][k]

    def step(self):
        route = []
        for i in range(self.pairs):
            route += [(self.at(i, 0), self.at(i + 1, 0)), (self.at(i, 1), self.at(i - 1, 1))]
        return route

    def sibling(self):
        return [(e, e ^ 1) for e in range(self.count)]

    def source(self, s, flip_lane, flip_way):
        out = []
        for e in range(self.count):
            i, k = self.place[e]
            way = 1 if k == 0 else -1
            if flip_way:
                way = -way
            out.append(self.at(i - s * way, k ^ flip_lane))
        return out


def swap_pairs(axis):
    count = lax.axis_size(axis)
    route = []
    for low in range(0, count - 1, 2):
        route += [(low, low + 1), (low + 1, low)]
    return route


def attend_body(first, count, len_ref, far_len_ref, q_ref, kv_ref, cache_ref, fk_ref, fv_ref, out_ref):
    rows = q_ref.shape[0]
    seg = fk_ref.shape[0]
    near_len = len_ref[0, 0]
    far_len = far_len_ref[0]
    pos = lax.broadcasted_iota(jnp.int32, (rows, seg), 1)
    near_ok = pos < near_len
    far_ok = pos < far_len
    scale = 1.0 / math.sqrt(HD)
    dims = (((1,), (1,)), ((), ()))
    for h in range(count):
        cols = slice((first + h) * HD, (first + h + 1) * HD)
        q = q_ref[:, cols]
        s0 = lax.dot_general(q, kv_ref[0, :, cols], dims, preferred_element_type=F32) * scale
        s1 = lax.dot_general(q, cache_ref[0, 0, 0, :, cols], dims, preferred_element_type=F32) * scale
        s2 = lax.dot_general(q, fk_ref[:, cols], dims, preferred_element_type=F32) * scale
        s1 = jnp.where(near_ok, s1, -1e30)
        s2 = jnp.where(far_ok, s2, -1e30)
        m = jnp.max(jnp.maximum(jnp.maximum(s0, s1), s2), axis=1, keepdims=True)
        w0 = jnp.exp(s0 - m)
        w1 = jnp.where(near_ok, jnp.exp(s1 - m), 0.0)
        w2 = jnp.where(far_ok, jnp.exp(s2 - m), 0.0)
        l = jnp.sum(w0 + w1 + w2, axis=1, keepdims=True)
        a = jnp.dot(w0.astype(BF16), kv_ref[1, :, cols], preferred_element_type=F32)
        a += jnp.dot(w1.astype(BF16), cache_ref[1, 0, 0, :, cols], preferred_element_type=F32)
        a += jnp.dot(w2.astype(BF16), fv_ref[:, cols], preferred_element_type=F32)
        out_ref[h] = (a / l).astype(BF16)


def full():
    return pl.BlockSpec(memory_space=pltpu.VMEM)


def scalars():
    return pl.BlockSpec(memory_space=SMEM)


def attend(first, count, queries, span_kv, cache_kv, far_k, far_v, seg_len, far_len):
    rows = queries.shape[0]
    return pl.pallas_call(
        functools.partial(attend_body, first, count),
        out_shape=jax.ShapeDtypeStruct((count, rows, HD), BF16),
        in_specs=[scalars(), scalars()] + [full()] * 5,
        out_specs=full(),
        cost_estimate=pl.CostEstimate(
            flops=40 * rows * rows * HD * count, bytes_accessed=16 * rows * HD * count, transcendentals=0
        ),
        compiler_params=pltpu.CompilerParams(vmem_limit_bytes=16 * 2**20),
        name="attend",
    )(seg_len, far_len, queries, span_kv, cache_kv, far_k, far_v)


def pack_body(count, lane_ref, rows_ref, routes_ref, wts_ref, own_ref, other_ref):
    slab, half = rows_ref.shape[0], own_ref.shape[1]
    lane = lane_ref[0]
    own_ref[:slab] = rows_ref[:, pl.ds(pl.multiple_of(lane * half, HD), half)]
    other_ref[:slab] = rows_ref[:, pl.ds(pl.multiple_of((1 - lane) * half, HD), half)]
    routes = routes_ref[...]
    wts = wts_ref[...]
    tokens = wts.shape[1]
    high, low = [], []
    for group in range(count // 8):
        dense = jnp.concatenate(
            [
                jnp.sum(jnp.where(routes == group * 8 + j, wts, 0.0), axis=0, keepdims=True)
                for j in range(8)
            ],
            axis=0,
        )
        top = dense.astype(BF16)
        high.append(top)
        low.append((dense - top.astype(F32)).astype(BF16))
    tail = jnp.concatenate(high + low, axis=1)
    for out in (own_ref, other_ref):
        out[slab:, : tail.shape[1]] = tail
        if tail.shape[1] < half:
            out[slab:, tail.shape[1] :] = jnp.zeros((8, half - tail.shape[1]), BF16)


def pack(count, lane, o_rows, routes, route_wts):
    slab, width = o_rows.shape
    out = jax.ShapeDtypeStruct((slab + 8, width // 2), BF16)
    return pl.pallas_call(
        functools.partial(pack_body, count),
        out_shape=(out, out),
        in_specs=[scalars()] + [full()] * 3,
        out_specs=(full(), full()),
        cost_estimate=pl.CostEstimate(flops=slab * width, bytes_accessed=4 * slab * width, transcendentals=0),
        compiler_params=pltpu.CompilerParams(vmem_limit_bytes=8 * 2**20),
        name="pack",
    )(lane, o_rows, routes.T, route_wts.T)


def project_body(first, blocks, pieces, carried, table_ref, me_ref, *refs):
    refs = list(refs)
    mine = [refs.pop(0) for _ in range(pieces)]
    theirs = [refs.pop(0) for _ in range(pieces)]
    before = [refs.pop(0) for _ in range(2 if carried else 0)]
    source = [refs.pop(0) for _ in range(blocks)]
    own_ref, give_ref, wts_ref, att, held, sems = refs
    rows = own_ref.shape[0]
    slab = att.shape[2]
    me = me_ref[0]
    copies = [pltpu.make_async_copy(source[b], held.at[b], sems.at[b]) for b in range(blocks)]
    for copy in copies:
        copy.start()
    at = 0
    for a, b in zip(mine, theirs):
        att[at : at + a.shape[0], :rows] = a[...]
        att[at : at + a.shape[0], rows:] = b[...]
        at += a.shape[0]
    sub, group = lax.rem(me, 8), me // 8
    groups = att.shape[0] // 8
    pick = lax.broadcasted_iota(jnp.int32, (8, rows), 0) == sub
    total = None
    lines = []
    for b in range(blocks):
        copies[b].wait()
        block = held[b, :slab]
        part = jnp.dot(att[table_ref[me, first + b]], block, preferred_element_type=F32)
        total = part if total is None else total + part
        high = held[b, slab:, pl.ds(pl.multiple_of(group * rows, 128), rows)].astype(F32)
        low = held[b, slab:, pl.ds(pl.multiple_of((groups + group) * rows, 128), rows)].astype(F32)
        lines.append(jnp.sum(jnp.where(pick, high + low, 0.0), axis=0, keepdims=True))
    if carried:
        own_ref[...] = before[0][...] + total[:rows]
        give_ref[...] = before[1][...] + total[rows:]
    else:
        own_ref[...] = total[:rows]
        give_ref[...] = total[rows:]
    lines.append(jnp.zeros((128 - blocks, rows), F32))
    wts_ref[...] = jnp.concatenate(lines, axis=0).T


def project(table, me, first, mine, theirs, before, blocks):
    count = sum(part.shape[0] for part in mine)
    rows, slab = mine[0].shape[1:]
    half = blocks[0].shape[1]
    out = jax.ShapeDtypeStruct((rows, half), F32)
    number = len(blocks)
    return pl.pallas_call(
        functools.partial(project_body, first, number, len(mine), bool(before)),
        out_shape=(out, out, jax.ShapeDtypeStruct((rows, 128), F32)),
        in_specs=[scalars(), scalars()]
        + [full()] * (2 * len(mine) + len(before))
        + [pl.BlockSpec(memory_space=pl.ANY)] * number,
        out_specs=(full(), full(), full()),
        scratch_shapes=[
            pltpu.VMEM((count, 2 * rows, slab), BF16),
            pltpu.VMEM((number,) + blocks[0].shape, BF16),
            pltpu.SemaphoreType.DMA((number,)),
        ],
        cost_estimate=pl.CostEstimate(
            flops=4 * rows * half * slab * number, bytes_accessed=2 * half * slab * number, transcendentals=0
        ),
        compiler_params=pltpu.CompilerParams(vmem_limit_bytes=20 * 2**20),
        name="project",
    )(table, me, *mine, *theirs, *before, *blocks)


def norm_body(lane_ref, resid_ref, own_ref, got_ref, gain_ref, sum_ref, out_ref):
    first = lane_ref[0] == 0
    half = own_ref.shape[1]
    own = own_ref[...]
    got = got_ref[...]
    low = resid_ref[:, :half].astype(F32) + jnp.where(first, own, got)
    high = resid_ref[:, half:].astype(F32) + jnp.where(first, got, own)
    sum_ref[:, :half] = low
    sum_ref[:, half:] = high
    square = jnp.sum(low * low + high * high, axis=1, keepdims=True)
    scale = lax.rsqrt(square * (1.0 / (2 * half)) + 1e-05)
    out_ref[:, :half] = (low * scale * gain_ref[:, :half]).astype(BF16)
    out_ref[:, half:] = (high * scale * gain_ref[:, half:]).astype(BF16)


def norm(lane, resid, own, got, gain):
    return pl.pallas_call(
        norm_body,
        out_shape=(
            jax.ShapeDtypeStruct(resid.shape, F32),
            jax.ShapeDtypeStruct(resid.shape, BF16),
        ),
        in_specs=[scalars()] + [full()] * 4,
        out_specs=(full(), full()),
        cost_estimate=pl.CostEstimate(
            flops=8 * resid.size, bytes_accessed=12 * resid.size, transcendentals=0
        ),
        compiler_params=pltpu.CompilerParams(vmem_limit_bytes=16 * 2**20),
        name="norm",
    )(lane, resid, own, got, gain.reshape(1, -1))


def expert_body(cols, xa_ref, xb_ref, ya_ref, yb_ref, wx_ref, wy_ref, in_ref, down_ref, cx_ref, cy_ref):
    rows, width = cx_ref.shape
    both = jnp.concatenate([xa_ref[...], xb_ref[...], ya_ref[...], yb_ref[...]], axis=0)
    gate = jnp.dot(both, in_ref[0, :, :FF], preferred_element_type=F32)
    up = jnp.dot(both, in_ref[0, :, FF:], preferred_element_type=F32)
    hidden = (gate * jax.nn.sigmoid(gate) * up).astype(BF16)
    wx = wx_ref[:, cols[0] : cols[0] + 1]
    wy = wy_ref[:, cols[1] : cols[1] + 1]
    step = 512
    for at in range(0, width, step):
        out = jnp.dot(hidden, down_ref[0, :, at : at + step], preferred_element_type=F32)
        cx_ref[:, at : at + step] = (out[:rows] * wx).astype(BF16)
        cy_ref[:, at : at + step] = (out[rows:] * wy).astype(BF16)


def expert(cols, x, y, wx, wy, w_in, w_out):
    rows, width = 2 * x[0].shape[0], x[0].shape[1]
    out = jax.ShapeDtypeStruct((rows, width), BF16)
    return pl.pallas_call(
        functools.partial(expert_body, cols),
        out_shape=(out, out),
        in_specs=[full()] * 8,
        out_specs=(full(), full()),
        cost_estimate=pl.CostEstimate(
            flops=12 * rows * width * FF, bytes_accessed=6 * width * FF, transcendentals=0
        ),
        compiler_params=pltpu.CompilerParams(vmem_limit_bytes=24 * 2**20),
        name="expert",
    )(*x, *y, wx, wy, w_in, w_out)


def shards(
    ring, resid, queries, span_kv, cache_kv, seg_len, o_rows, norm_gain, routes, route_wts, w_in, w_out
):
    count, pairs = ring.count, ring.pairs
    rows, width = queries.shape
    me = lax.axis_index("expert")
    lane = me % 2
    forward, sibling = ring.step(), ring.sibling()

    def ahead(block):
        return lax.ppermute(block, "expert", forward)

    def across(block):
        return lax.ppermute(block, "expert", sibling)

    group_swap = swap_pairs("group")
    far_len = lax.ppermute(seg_len[0, 1:2], "group", group_swap)
    far_k = lax.ppermute(cache_kv[0, 0, 1], "group", group_swap)
    far_v = lax.ppermute(cache_kv[1, 0, 1], "group", group_swap)

    chain_a, other = pack(count, lane[None], o_rows, routes, route_wts)
    chain_b = across(other)
    blocks = [chain_a, chain_b]
    for s in range(1, pairs):
        chain_a = ahead(chain_a)
        chain_b = ahead(chain_b)
        blocks += [chain_a, chain_b]
    sources = []
    for s in range(pairs):
        sources += [ring.source(s, 0, False), ring.source(s, 1, False)]
    table = jnp.asarray([[line[e] for line in sources] for e in range(count)], jnp.int32)

    mine, theirs = [], []
    for first in range(0, HEADS, HEADS // 2):
        part = attend(first, HEADS // 2, queries, span_kv, cache_kv, far_k, far_v, seg_len, far_len)
        mine.append(part)
        theirs.append(across(part))
    slab = o_rows.shape[0]
    if slab != HD:
        mine, theirs = (
            [jnp.concatenate(p).transpose(1, 0, 2).reshape(rows, count, slab).transpose(1, 0, 2)]
            for p in (mine, theirs)
        )
    early = 2 * (pairs * 5 // 8)
    first_own, first_give, wts_early = project(table, me[None], 0, mine, theirs, [], blocks[:early])
    own, give, wts_late = project(
        table, me[None], early, mine, theirs, [first_own, first_give], blocks[early:]
    )
    got = across(give)
    residual, normed = norm(lane[None], resid, own, got, norm_gain)

    def gate_at(column):
        return (wts_early, column) if column < early else (wts_late, column - early)

    part_rows = rows // 2
    x = [normed[:part_rows], normed[part_rows:]]
    y = [across(p) for p in x]
    travelling = None
    for s in range(pairs):
        wx, column_x = gate_at(2 * s)
        wy, column_y = gate_at(2 * ((pairs - s) % pairs) + 1)
        keep, give = expert((column_x, column_y), x, y, wx, wy, w_in, w_out)
        back = across(give)
        if s == 0:
            total = residual + keep.astype(F32) + back.astype(F32)
        else:
            part = [
                keep[at : at + part_rows].astype(F32) + back[at : at + part_rows].astype(F32)
                for at in (0, part_rows)
            ]
            if travelling is not None:
                part = [p + t.astype(F32) for p, t in zip(part, travelling)]
            travelling = [ahead(p.astype(BF16)) for p in part]
        if s + 1 < pairs:
            x = [ahead(p) for p in x]
            y = [across(p) for p in x]
    out = [
        total[i * part_rows : (i + 1) * part_rows] + t.astype(F32) for i, t in enumerate(travelling)
    ]
    return jnp.concatenate(out, axis=0).astype(BF16)


def solution(mesh):
    placed = (
        P(("group", "expert"), None),
        P(("group", "expert"), None),
        P(None, ("group", "expert"), None),
        P(None, ("group", "expert"), None, None, None),
        P(("group", "expert"), None),
        P("expert", None),
        P(),
        P(("group", "expert"), None),
        P(("group", "expert"), None),
        P("expert", None, None),
        P("expert", None, None),
    )
    ring = Ring(mesh.shape["expert"])
    return jax.shard_map(
        functools.partial(shards, ring),
        mesh=mesh,
        in_specs=placed,
        out_specs=P(("group", "expert"), None),
        check_vma=False,
    )
```

```python
import functools
import math

import jax
import jax.numpy as jnp
from jax import lax
from jax.experimental import pallas as pl
from jax.experimental.pallas import tpu as pltpu
from jax.sharding import PartitionSpec as P

HEADS = 16
HD = 128
FF = 512
F32 = jnp.float32
BF16 = jnp.bfloat16
SMEM = pltpu.SMEM


class Ring:
    def __init__(self, count):
        self.count = count
        self.pairs = count // 2
        chips = list(range(0, self.pairs, 2)) + list(range(1, self.pairs, 2))[::-1]
        self.device = [[2 * c, 2 * c + 1] for c in chips]
        self.place = {self.device[i][k]: (i, k) for i in range(self.pairs) for k in (0, 1)}

    def at(self, i, k):
        return self.device[i % self.pairs][k]

    def step(self):
        route = []
        for i in range(self.pairs):
            route += [(self.at(i, 0), self.at(i + 1, 0)), (self.at(i, 1), self.at(i - 1, 1))]
        return route

    def sibling(self):
        return [(e, e ^ 1) for e in range(self.count)]

    def source(self, s, flip_lane, flip_way):
        out = []
        for e in range(self.count):
            i, k = self.place[e]
            way = 1 if k == 0 else -1
            if flip_way:
                way = -way
            out.append(self.at(i - s * way, k ^ flip_lane))
        return out


def swap_pairs(axis):
    count = lax.axis_size(axis)
    route = []
    for low in range(0, count - 1, 2):
        route += [(low, low + 1), (low + 1, low)]
    return route


def attend_body(first, count, len_ref, far_len_ref, q_ref, kv_ref, cache_ref, far_ref, held_ref, out_ref, pass_ref):
    del held_ref, pass_ref
    rows = q_ref.shape[0]
    seg = far_ref.shape[1]
    near_len = len_ref[0, 0]
    far_len = far_len_ref[0]
    pos = lax.broadcasted_iota(jnp.int32, (rows, seg), 1)
    near_ok = pos < near_len
    far_ok = pos < far_len
    scale = 1.0 / math.sqrt(HD)
    dims = (((1,), (1,)), ((), ()))
    for h in range(count):
        cols = slice((first + h) * HD, (first + h + 1) * HD)
        far_cols = slice(h * HD, (h + 1) * HD)
        q = q_ref[:, cols]
        s0 = lax.dot_general(q, kv_ref[0, :, cols], dims, preferred_element_type=F32) * scale
        s1 = lax.dot_general(q, cache_ref[0, 0, 0, :, cols], dims, preferred_element_type=F32) * scale
        s2 = lax.dot_general(q, far_ref[0, :, far_cols], dims, preferred_element_type=F32) * scale
        s1 = jnp.where(near_ok, s1, -1e30)
        s2 = jnp.where(far_ok, s2, -1e30)
        m = jnp.max(jnp.maximum(jnp.maximum(s0, s1), s2), axis=1, keepdims=True)
        w0 = jnp.exp(s0 - m)
        w1 = jnp.where(near_ok, jnp.exp(s1 - m), 0.0)
        w2 = jnp.where(far_ok, jnp.exp(s2 - m), 0.0)
        l = jnp.sum(w0 + w1 + w2, axis=1, keepdims=True)
        a = jnp.dot(w0.astype(BF16), kv_ref[1, :, cols], preferred_element_type=F32)
        a += jnp.dot(w1.astype(BF16), cache_ref[1, 0, 0, :, cols], preferred_element_type=F32)
        a += jnp.dot(w2.astype(BF16), far_ref[1, :, far_cols], preferred_element_type=F32)
        out_ref[h] = (a / l).astype(BF16)


def full():
    return pl.BlockSpec(memory_space=pltpu.VMEM)


def scalars():
    return pl.BlockSpec(memory_space=SMEM)


def anywhere():
    return pl.BlockSpec(memory_space=pl.ANY)


def attend(first, count, queries, span_kv, cache_kv, far, seg_len, far_len, held):
    rows = queries.shape[0]
    return pl.pallas_call(
        functools.partial(attend_body, first, count),
        out_shape=(
            jax.ShapeDtypeStruct((count, rows, HD), BF16),
            jax.ShapeDtypeStruct(held.shape, held.dtype),
        ),
        in_specs=[scalars(), scalars()] + [full()] * 4 + [anywhere()],
        out_specs=(full(), anywhere()),
        input_output_aliases={6: 1},
        cost_estimate=pl.CostEstimate(
            flops=40 * rows * rows * HD * count, bytes_accessed=16 * rows * HD * count, transcendentals=0
        ),
        compiler_params=pltpu.CompilerParams(vmem_limit_bytes=16 * 2**20),
        name="attend",
    )(seg_len, far_len, queries, span_kv, cache_kv, far, held)


def pack_body(count, lane_ref, rows_ref, routes_ref, wts_ref, own_ref, other_ref):
    slab, half = rows_ref.shape[0], own_ref.shape[1]
    lane = lane_ref[0]
    own_ref[:slab] = rows_ref[:, pl.ds(pl.multiple_of(lane * half, HD), half)]
    other_ref[:slab] = rows_ref[:, pl.ds(pl.multiple_of((1 - lane) * half, HD), half)]
    routes = routes_ref[...]
    wts = wts_ref[...]
    tokens = wts.shape[1]
    high, low = [], []
    for group in range(count // 8):
        dense = jnp.concatenate(
            [
                jnp.sum(jnp.where(routes == group * 8 + j, wts, 0.0), axis=0, keepdims=True)
                for j in range(8)
            ],
            axis=0,
        )
        top = dense.astype(BF16)
        high.append(top)
        low.append((dense - top.astype(F32)).astype(BF16))
    tail = jnp.concatenate(high + low, axis=1)
    for out in (own_ref, other_ref):
        out[slab:, : tail.shape[1]] = tail
        if tail.shape[1] < half:
            out[slab:, tail.shape[1] :] = jnp.zeros((8, half - tail.shape[1]), BF16)


def pack(count, lane, o_rows, routes, route_wts):
    slab, width = o_rows.shape
    out = jax.ShapeDtypeStruct((slab + 8, width // 2), BF16)
    return pl.pallas_call(
        functools.partial(pack_body, count),
        out_shape=(out, out),
        in_specs=[scalars()] + [full()] * 3,
        out_specs=(full(), full()),
        cost_estimate=pl.CostEstimate(flops=slab * width, bytes_accessed=4 * slab * width, transcendentals=0),
        compiler_params=pltpu.CompilerParams(vmem_limit_bytes=8 * 2**20),
        name="pack",
    )(lane, o_rows, routes.T, route_wts.T)


def project_body(first, blocks, pieces, carried, table_ref, me_ref, *refs):
    refs = list(refs)
    mine = [refs.pop(0) for _ in range(pieces)]
    theirs = [refs.pop(0) for _ in range(pieces)]
    before = [refs.pop(0) for _ in range(2 if carried else 0)]
    source = [refs.pop(0) for _ in range(blocks)]
    own_ref, give_ref, wts_ref, att, held, sems = refs
    rows = own_ref.shape[0]
    slab = att.shape[2]
    me = me_ref[0]
    copies = [pltpu.make_async_copy(source[b], held.at[b], sems.at[b]) for b in range(blocks)]
    for copy in copies:
        copy.start()
    at = 0
    for a, b in zip(mine, theirs):
        att[at : at + a.shape[0], :rows] = a[...]
        att[at : at + a.shape[0], rows:] = b[...]
        at += a.shape[0]
    sub, group = lax.rem(me, 8), me // 8
    groups = att.shape[0] // 8
    pick = lax.broadcasted_iota(jnp.int32, (8, rows), 0) == sub
    total = None
    lines = []
    for b in range(blocks):
        copies[b].wait()
        block = held[b, :slab]
        part = jnp.dot(att[table_ref[me, first + b]], block, preferred_element_type=F32)
        total = part if total is None else total + part
        high = held[b, slab:, pl.ds(pl.multiple_of(group * rows, 128), rows)].astype(F32)
        low = held[b, slab:, pl.ds(pl.multiple_of((groups + group) * rows, 128), rows)].astype(F32)
        lines.append(jnp.sum(jnp.where(pick, high + low, 0.0), axis=0, keepdims=True))
    if carried:
        own_ref[...] = before[0][...] + total[:rows]
        give_ref[...] = before[1][...] + total[rows:]
    else:
        own_ref[...] = total[:rows]
        give_ref[...] = total[rows:]
    lines.append(jnp.zeros((128 - blocks, rows), F32))
    wts_ref[...] = jnp.concatenate(lines, axis=0).T


def project(table, me, first, mine, theirs, before, blocks):
    count = sum(part.shape[0] for part in mine)
    rows, slab = mine[0].shape[1:]
    half = blocks[0].shape[1]
    out = jax.ShapeDtypeStruct((rows, half), F32)
    number = len(blocks)
    return pl.pallas_call(
        functools.partial(project_body, first, number, len(mine), bool(before)),
        out_shape=(out, out, jax.ShapeDtypeStruct((rows, 128), F32)),
        in_specs=[scalars(), scalars()]
        + [full()] * (2 * len(mine) + len(before))
        + [pl.BlockSpec(memory_space=pl.ANY)] * number,
        out_specs=(full(), full(), full()),
        scratch_shapes=[
            pltpu.VMEM((count, 2 * rows, slab), BF16),
            pltpu.VMEM((number,) + blocks[0].shape, BF16),
            pltpu.SemaphoreType.DMA((number,)),
        ],
        cost_estimate=pl.CostEstimate(
            flops=4 * rows * half * slab * number, bytes_accessed=2 * half * slab * number, transcendentals=0
        ),
        compiler_params=pltpu.CompilerParams(vmem_limit_bytes=20 * 2**20),
        name="project",
    )(table, me, *mine, *theirs, *before, *blocks)


def norm_body(lane_ref, resid_ref, own_ref, got_ref, gain_ref, sum_ref, out_ref):
    first = lane_ref[0] == 0
    half = own_ref.shape[1]
    own = own_ref[...]
    got = got_ref[...]
    low = resid_ref[:, :half].astype(F32) + jnp.where(first, own, got)
    high = resid_ref[:, half:].astype(F32) + jnp.where(first, got, own)
    sum_ref[:, :half] = low
    sum_ref[:, half:] = high
    square = jnp.sum(low * low + high * high, axis=1, keepdims=True)
    scale = lax.rsqrt(square * (1.0 / (2 * half)) + 1e-05)
    out_ref[:, :half] = (low * scale * gain_ref[:, :half]).astype(BF16)
    out_ref[:, half:] = (high * scale * gain_ref[:, half:]).astype(BF16)


def norm(lane, resid, own, got, gain):
    return pl.pallas_call(
        norm_body,
        out_shape=(
            jax.ShapeDtypeStruct(resid.shape, F32),
            jax.ShapeDtypeStruct(resid.shape, BF16),
        ),
        in_specs=[scalars()] + [full()] * 4,
        out_specs=(full(), full()),
        cost_estimate=pl.CostEstimate(
            flops=8 * resid.size, bytes_accessed=12 * resid.size, transcendentals=0
        ),
        compiler_params=pltpu.CompilerParams(vmem_limit_bytes=16 * 2**20),
        name="norm",
    )(lane, resid, own, got, gain.reshape(1, -1))


def expert_body(cols, after, *refs):
    refs = list(refs)
    x_ref, y_ref, wx_ref, wy_ref, in_ref, down_ref = refs[:6]
    cx_ref, cy_ref = refs[6 + after :]
    rows, width = cx_ref.shape
    both = jnp.concatenate([x_ref[...], y_ref[...]], axis=0)
    gate = jnp.dot(both, in_ref[0, :, :FF], preferred_element_type=F32)
    up = jnp.dot(both, in_ref[0, :, FF:], preferred_element_type=F32)
    hidden = (gate * jax.nn.sigmoid(gate) * up).astype(BF16)
    wx = wx_ref[:, cols[0] : cols[0] + 1]
    wy = wy_ref[:, cols[1] : cols[1] + 1]
    step = 512
    for at in range(0, width, step):
        out = jnp.dot(hidden, down_ref[0, :, at : at + step], preferred_element_type=F32)
        cx_ref[:, at : at + step] = (out[:rows] * wx).astype(BF16)
        cy_ref[:, at : at + step] = (out[rows:] * wy).astype(BF16)


def expert(cols, x, y, wx, wy, w_in, w_out, after=()):
    rows, width = x.shape
    out = jax.ShapeDtypeStruct((rows, width), BF16)
    return pl.pallas_call(
        functools.partial(expert_body, cols, len(after)),
        out_shape=(out, out),
        in_specs=[full()] * 6 + [anywhere()] * len(after),
        out_specs=(full(), full()),
        cost_estimate=pl.CostEstimate(
            flops=12 * rows * width * FF, bytes_accessed=6 * width * FF, transcendentals=0
        ),
        compiler_params=pltpu.CompilerParams(vmem_limit_bytes=24 * 2**20),
        name="expert",
    )(x, y, wx, wy, w_in, w_out, *after)


def add_body(*refs):
    total = refs[0][...].astype(F32)
    for ref in refs[1:-1]:
        total = total + ref[...].astype(F32)
    refs[-1][...] = total.astype(BF16)


def add(*terms):
    size = terms[0].size
    return pl.pallas_call(
        add_body,
        out_shape=jax.ShapeDtypeStruct(terms[0].shape, BF16),
        in_specs=[full()] * len(terms),
        out_specs=full(),
        cost_estimate=pl.CostEstimate(
            flops=len(terms) * size, bytes_accessed=4 * len(terms) * size, transcendentals=0
        ),
        compiler_params=pltpu.CompilerParams(vmem_limit_bytes=8 * 2**20),
        name="add",
    )(*terms)


def shards(
    ring, resid, queries, span_kv, cache_kv, seg_len, o_rows, norm_gain, routes, route_wts, w_in, w_out
):
    count, pairs = ring.count, ring.pairs
    rows, width = queries.shape
    me = lax.axis_index("expert")
    lane = me % 2
    forward, sibling = ring.step(), ring.sibling()

    def ahead(block):
        return lax.ppermute(block, "expert", forward)

    def across(block):
        return lax.ppermute(block, "expert", sibling)

    group_swap = swap_pairs("group")
    groups = 4
    heads = HEADS // groups
    wide = heads * HD
    far_len = lax.ppermute(seg_len[0, 1:2], "group", group_swap)
    far = [
        lax.ppermute(cache_kv[:, 0, 1, :, j * wide : (j + 1) * wide], "group", group_swap)
        for j in range(groups)
    ]

    chain_a, other = pack(count, lane[None], o_rows, routes, route_wts)
    chain_b = across(other)
    blocks = [chain_a, chain_b]
    mine, theirs = [], []
    for s in range(1, pairs):
        chain_a = ahead(chain_a)
        chain_b = ahead(chain_b)
        if len(mine) < groups:
            j = len(mine)
            part, chain_a = attend(
                j * heads, heads, queries, span_kv, cache_kv, far[j], seg_len, far_len, chain_a
            )
            mine.append(part)
            theirs.append(across(part))
        blocks += [chain_a, chain_b]
    sources = []
    for s in range(pairs):
        sources += [ring.source(s, 0, False), ring.source(s, 1, False)]
    table = jnp.asarray([[line[e] for line in sources] for e in range(count)], jnp.int32)

    slab = o_rows.shape[0]
    if slab != HD:
        mine, theirs = (
            [jnp.concatenate(p).transpose(1, 0, 2).reshape(rows, count, slab).transpose(1, 0, 2)]
            for p in (mine, theirs)
        )
    early = 2 * (pairs * 5 // 8)
    first_own, first_give, wts_early = project(table, me[None], 0, mine, theirs, [], blocks[:early])
    own, give, wts_late = project(
        table, me[None], early, mine, theirs, [first_own, first_give], blocks[early:]
    )
    got = across(give)
    residual, normed = norm(lane[None], resid, own, got, norm_gain)

    def gate_at(column):
        return (wts_early, column) if column < early else (wts_late, column - early)

    x = [normed]
    y = [across(normed)]
    for s in range(1, pairs):
        x.append(ahead(x[-1]))
        y.append(across(x[-1]))

    def sums(s, after=()):
        wx, column_x = gate_at(2 * s)
        wy, column_y = gate_at(2 * ((pairs - s) % pairs) + 1)
        keep, give = expert((column_x, column_y), x[s], y[s], wx, wy, w_in, w_out, after)
        return keep, across(give)

    travelling = ()
    for s in range(1, pairs):
        travelling = (ahead(add(*sums(s), *travelling)),)
    return add(residual, *sums(0, (x[min(3, pairs - 1)],)), *travelling)


def solution(mesh):
    placed = (
        P(("group", "expert"), None),
        P(("group", "expert"), None),
        P(None, ("group", "expert"), None),
        P(None, ("group", "expert"), None, None, None),
        P(("group", "expert"), None),
        P("expert", None),
        P(),
        P(("group", "expert"), None),
        P(("group", "expert"), None),
        P("expert", None, None),
        P("expert", None, None),
    )
    ring = Ring(mesh.shape["expert"])
    return jax.shard_map(
        functools.partial(shards, ring),
        mesh=mesh,
        in_specs=placed,
        out_specs=P(("group", "expert"), None),
        check_vma=False,
    )
```

```python
import functools
import math

import jax
import jax.numpy as jnp
from jax import lax
from jax.experimental import pallas as pl
from jax.experimental.pallas import tpu as pltpu
from jax.sharding import PartitionSpec as P

HEADS = 16
HD = 128
FF = 512
HOPS_X = 1
HELD = 4
AFTER = {3:0}
TAIL = 5
DEAD = 128.0
FAR_MIB = 60
ATT_MIB = 8
PRO_MIB = 14
EXP_MIB = 16
SPEED = 6.0
F32 = jnp.float32
BF16 = jnp.bfloat16
SMEM = pltpu.SMEM


class Ring:
    def __init__(self, groups, count):
        self.groups, self.count = groups, count
        self.pairs = count // 2
        chips = list(range(0, self.pairs, 2)) + list(range(1, self.pairs, 2))[::-1]
        self.device = [[2 * c, 2 * c + 1] for c in chips]
        self.place = {self.device[i][k]: (i, k) for i in range(self.pairs) for k in (0, 1)}

    def at(self, i, k):
        return self.device[i % self.pairs][k]

    def way(self, g, k):
        return 1 if (g + k) % 2 == 0 else -1

    def step(self, sign):
        route = []
        for g in range(self.groups):
            for e, (i, k) in self.place.items():
                target = self.at(i + sign * self.way(g, k), k)
                route.append((g * self.count + e, g * self.count + target))
        return route

    def sibling(self):
        return [(e, e ^ 1) for e in range(self.count)]

    def source(self, s, flip_lane):
        out = []
        for g in (0, 1):
            for e in range(self.count):
                i, k = self.place[e]
                out.append(self.at(i - s * self.way(g, k), k ^ flip_lane))
        return out


def swap_pairs(axis):
    count = lax.axis_size(axis)
    route = []
    for low in range(0, count - 1, 2):
        route += [(low, low + 1), (low + 1, low)]
    return route


def attend_body(first, count, after, len_ref, q_ref, kv_ref, cache_ref, far_ref, *refs):
    out_ref = refs[after]
    rows = q_ref.shape[0]
    seg = far_ref.shape[1]
    dims = (((1,), (1,)), ((), ()))
    unit = (lax.broadcasted_iota(jnp.int32, (rows, HD), 1) == 0).astype(BF16)
    mark = lax.dot_general(unit, far_ref[0, :, :HD], dims, preferred_element_type=F32)
    near_ok = lax.broadcasted_iota(jnp.int32, (rows, seg), 1) < len_ref[0, 0]
    far_ok = mark < DEAD / 2
    scale = 1.0 / math.sqrt(HD)
    for h in range(count):
        cols = slice((first + h) * HD, (first + h + 1) * HD)
        q = q_ref[:, cols]
        s0 = lax.dot_general(q, kv_ref[0, :, cols], dims, preferred_element_type=F32) * scale
        s1 = lax.dot_general(q, cache_ref[0, 0, 0, :, cols], dims, preferred_element_type=F32) * scale
        s2 = lax.dot_general(q, far_ref[0, :, cols], dims, preferred_element_type=F32) * scale
        s1 = jnp.where(near_ok, s1, -1e30)
        s2 = jnp.where(far_ok, s2, -1e30)
        m = jnp.max(jnp.maximum(jnp.maximum(s0, s1), s2), axis=1, keepdims=True)
        w0 = jnp.exp(s0 - m)
        w1 = jnp.where(near_ok, jnp.exp(s1 - m), 0.0)
        w2 = jnp.where(far_ok, jnp.exp(s2 - m), 0.0)
        l = jnp.sum(w0 + w1 + w2, axis=1, keepdims=True)
        a = jnp.dot(w0.astype(BF16), kv_ref[1, :, cols], preferred_element_type=F32)
        a += jnp.dot(w1.astype(BF16), cache_ref[1, 0, 0, :, cols], preferred_element_type=F32)
        a += jnp.dot(w2.astype(BF16), far_ref[1, :, cols], preferred_element_type=F32)
        out_ref[h] = (a / l).astype(BF16)


def far_body(len_ref, cache_ref, out_ref, sems):
    copies = [pltpu.make_async_copy(cache_ref.at[i, 0, 1], out_ref.at[i], sems.at[i]) for i in (0, 1)]
    for copy in copies:
        copy.start()
    for copy in copies:
        copy.wait()
    row = lax.broadcasted_iota(jnp.int32, out_ref.shape[1:], 0)
    out_ref[0] = jnp.where(row < len_ref[0, 1], out_ref[0].astype(F32), DEAD).astype(BF16)


def far_segment(seg_len, cache_kv):
    return pl.pallas_call(
        far_body,
        out_shape=jax.ShapeDtypeStruct((2,) + cache_kv.shape[3:], BF16),
        in_specs=[scalars(), in_hbm()],
        out_specs=full(),
        scratch_shapes=[pltpu.SemaphoreType.DMA((2,))],
        cost_estimate=cost(1.7),
        compiler_params=pltpu.CompilerParams(vmem_limit_bytes=FAR_MIB * 2**20),
        name="far_segment",
    )(seg_len, cache_kv)


def cost(micros):
    return pl.CostEstimate(flops=int(micros * 1e9 * SPEED), bytes_accessed=1000, transcendentals=0)


def full():
    return pl.BlockSpec(memory_space=pltpu.VMEM)


def scalars():
    return pl.BlockSpec(memory_space=SMEM)


def in_hbm():
    return pl.BlockSpec(memory_space=pltpu.HBM)


def anywhere():
    return pl.BlockSpec(memory_space=pl.ANY)


def attend(first, count, queries, span_kv, cache_kv, far, seg_len, held=None, after=()):
    rows = queries.shape[0]
    out = [jax.ShapeDtypeStruct((count, rows, HD), BF16)]
    passed = [] if held is None else [held]
    out += [jax.ShapeDtypeStruct(p.shape, p.dtype) for p in passed]
    return pl.pallas_call(
        functools.partial(attend_body, first, count, len(passed) + len(after)),
        out_shape=out,
        in_specs=[scalars()] + [full()] * 4 + [anywhere()] * (len(passed) + len(after)),
        out_specs=[full()] + [anywhere()] * len(passed),
        input_output_aliases={5: 1} if passed else {},
        cost_estimate=cost(2.4),
        compiler_params=pltpu.CompilerParams(vmem_limit_bytes=ATT_MIB * 2**20),
        name="attend",
    )(seg_len, queries, span_kv, cache_kv, far, *passed, *after)


def pack_body(count, lane_ref, rows_ref, routes_ref, wts_ref, own_ref, other_ref):
    slab, half = rows_ref.shape[0], own_ref.shape[1]
    lane = lane_ref[0]
    own_ref[:slab] = rows_ref[:, pl.ds(pl.multiple_of(lane * half, HD), half)]
    other_ref[:slab] = rows_ref[:, pl.ds(pl.multiple_of((1 - lane) * half, HD), half)]
    routes = routes_ref[...]
    wts = wts_ref[...]
    tokens = wts.shape[1]
    high, low = [], []
    for group in range(count // 8):
        dense = jnp.concatenate(
            [
                jnp.sum(jnp.where(routes == group * 8 + j, wts, 0.0), axis=0, keepdims=True)
                for j in range(8)
            ],
            axis=0,
        )
        top = dense.astype(BF16)
        high.append(top)
        low.append((dense - top.astype(F32)).astype(BF16))
    tail = jnp.concatenate(high + low, axis=1)
    for out in (own_ref, other_ref):
        out[slab:, : tail.shape[1]] = tail
        if tail.shape[1] < half:
            out[slab:, tail.shape[1] :] = jnp.zeros((8, half - tail.shape[1]), BF16)


def pack(count, lane, o_rows, routes, route_wts):
    slab, width = o_rows.shape
    out = jax.ShapeDtypeStruct((slab + 8, width // 2), BF16)
    return pl.pallas_call(
        functools.partial(pack_body, count),
        out_shape=(out, out),
        in_specs=[scalars()] + [full()] * 3,
        out_specs=(full(), full()),
        cost_estimate=cost(0.7),
        compiler_params=pltpu.CompilerParams(vmem_limit_bytes=8 * 2**20),
        name="pack",
    )(lane, o_rows, routes.T, route_wts.T)


def project_body(first, blocks, pieces, carried, here, tail, table_ref, me_ref, *refs):
    refs = list(refs)
    mine = [refs.pop(0) for _ in range(pieces)]
    theirs = [refs.pop(0) for _ in range(pieces)]
    before = [refs.pop(0) for _ in range(2 if carried else 0)]
    source = [refs.pop(0) for _ in range(blocks)]
    tail_refs = [refs.pop(0) for _ in range(tail // 2)]
    own_ref, give_ref, wts_ref, att = refs[:4]
    rows = own_ref.shape[0]
    slab = att.shape[2]
    count = att.shape[0]
    copies = []
    if here < blocks:
        held, sems = refs[4:]
        away = range(blocks - here)
        copies = [pltpu.make_async_copy(source[b], held.at[b], sems.at[b]) for b in away]
        for copy in copies:
            copy.start()
        source = [held.at[b] for b in away] + source[blocks - here :]
    at = 0
    for a, b in zip(mine, theirs):
        att[at : at + a.shape[0], :rows] = a[...]
        att[at : at + a.shape[0], rows:] = b[...]
        at += a.shape[0]
    place = me_ref[0]
    me = lax.rem(place, count)
    sub, group = lax.rem(me, 8), me // 8
    groups = count // 8
    pick = lax.broadcasted_iota(jnp.int32, (8, rows), 0) == sub

    def line(ref, at):
        high = ref[at : at + 8, pl.ds(pl.multiple_of(group * rows, 128), rows)].astype(F32)
        low = ref[at : at + 8, pl.ds(pl.multiple_of((groups + group) * rows, 128), rows)].astype(F32)
        return jnp.sum(jnp.where(pick, high + low, 0.0), axis=0, keepdims=True)

    total = None
    lines = [None] * blocks
    for b in [*range(blocks - here, blocks), *range(blocks - here)]:
        if b < len(copies):
            copies[b].wait()
        head = att[table_ref[place, first + b]]
        part = jnp.dot(head, source[b][:slab], preferred_element_type=F32)
        total = part if total is None else total + part
        if b >= tail:
            lines[b] = line(source[b], slab)
    for i, ref in enumerate(tail_refs):
        lines[2 * i : 2 * i + 2] = [line(ref, 0), line(ref, 8)]
    if carried:
        own_ref[...] = before[0][...] + total[:rows]
        give_ref[...] = before[1][...] + total[rows:]
    else:
        own_ref[...] = total[:rows]
        give_ref[...] = total[rows:]
    lines.append(jnp.zeros((128 - blocks, rows), F32))
    wts_ref[...] = jnp.concatenate(lines, axis=0).T


def project(table, place, first, mine, theirs, before, blocks, here, tails=()):
    count = sum(part.shape[0] for part in mine)
    rows, slab = mine[0].shape[1:]
    half = blocks[0].shape[1]
    out = jax.ShapeDtypeStruct((rows, half), F32)
    number = len(blocks)
    scratch = [pltpu.VMEM((count, 2 * rows, slab), BF16)]
    away = number - here
    if away:
        scratch += [pltpu.VMEM((away,) + blocks[0].shape, BF16), pltpu.SemaphoreType.DMA((away,))]
    return pl.pallas_call(
        functools.partial(
            project_body, first, number, len(mine), bool(before), here, 2 * len(tails)
        ),
        out_shape=(out, out, jax.ShapeDtypeStruct((rows, 128), F32)),
        in_specs=[scalars(), scalars()]
        + [full()] * (2 * len(mine) + len(before))
        + [in_hbm()] * away
        + [full()] * here
        + [full()] * len(tails),
        out_specs=(full(), full(), full()),
        scratch_shapes=scratch,
        cost_estimate=pl.CostEstimate(
            flops=4 * rows * half * slab * number, bytes_accessed=2 * half * slab * number, transcendentals=0
        ),
        compiler_params=pltpu.CompilerParams(vmem_limit_bytes=PRO_MIB * 2**20),
        name="project",
    )(table, place, *mine, *theirs, *before, *blocks, *tails)


def norm_body(lane_ref, resid_ref, own_ref, got_ref, gain_ref, sum_ref, out_ref):
    first = lane_ref[0] == 0
    half = own_ref.shape[1]
    own = own_ref[...]
    got = got_ref[...]
    low = resid_ref[:, :half].astype(F32) + jnp.where(first, own, got)
    high = resid_ref[:, half:].astype(F32) + jnp.where(first, got, own)
    sum_ref[:, :half] = low
    sum_ref[:, half:] = high
    square = jnp.sum(low * low + high * high, axis=1, keepdims=True)
    scale = lax.rsqrt(square * (1.0 / (2 * half)) + 1e-05)
    out_ref[:, :half] = (low * scale * gain_ref[:, :half]).astype(BF16)
    out_ref[:, half:] = (high * scale * gain_ref[:, half:]).astype(BF16)


def norm(lane, resid, own, got, gain):
    return pl.pallas_call(
        norm_body,
        out_shape=(
            jax.ShapeDtypeStruct(resid.shape, F32),
            jax.ShapeDtypeStruct(resid.shape, BF16),
        ),
        in_specs=[scalars()] + [full()] * 4,
        out_specs=(full(), full()),
        cost_estimate=cost(0.4),
        compiler_params=pltpu.CompilerParams(vmem_limit_bytes=16 * 2**20),
        name="norm",
    )(lane, resid, own, got, gain.reshape(1, -1))


def expert_body(cols, parts, after, *refs):
    refs = list(refs)
    xy, (wx_ref, wy_ref, in_ref, down_ref) = refs[: 2 * parts], refs[2 * parts : 2 * parts + 4]
    cx_ref, *cy_refs = refs[2 * parts + 4 + after :]
    rows, width = cx_ref.shape
    size = rows // parts
    both = jnp.concatenate([ref[...] for ref in xy], axis=0)
    gate = jnp.dot(both, in_ref[0, :, :FF], preferred_element_type=F32)
    up = jnp.dot(both, in_ref[0, :, FF:], preferred_element_type=F32)
    hidden = (gate * jax.nn.sigmoid(gate) * up).astype(BF16)
    wx = wx_ref[:, cols[0] : cols[0] + 1]
    wy = wy_ref[:, cols[1] : cols[1] + 1]
    step = 512
    for at in range(0, width, step):
        out = jnp.dot(hidden, down_ref[0, :, at : at + step], preferred_element_type=F32)
        cx_ref[:, at : at + step] = (out[:rows] * wx).astype(BF16)
        cy = (out[rows:] * wy).astype(BF16)
        for i, cy_ref in enumerate(cy_refs):
            cy_ref[:, at : at + step] = cy[i * size : (i + 1) * size]


def expert(cols, x, y, wx, wy, w_in, w_out, after=()):
    rows, width = wx.shape[0], w_out.shape[2]
    parts = len(x)
    out = jax.ShapeDtypeStruct((rows, width), BF16)
    part = jax.ShapeDtypeStruct((rows // parts, width), BF16)
    return pl.pallas_call(
        functools.partial(expert_body, cols, parts, len(after)),
        out_shape=(out,) + (part,) * parts,
        in_specs=[full()] * (2 * parts + 4) + [anywhere()] * len(after),
        out_specs=(full(),) * (1 + parts),
        cost_estimate=cost(1.9),
        compiler_params=pltpu.CompilerParams(vmem_limit_bytes=EXP_MIB * 2**20),
        name="expert",
    )(*x, *y, wx, wy, w_in, w_out, *after)


def add_body(cuts, *refs):
    total = None
    at = 0
    for cut in cuts:
        term = jnp.concatenate([ref[c].astype(F32) for ref, c in zip(refs[at:], cut)], axis=0)
        at += len(cut)
        total = term if total is None else total + term
    refs[-1][...] = total.astype(BF16)


def add(cut, rows, terms):
    used, cuts = [], []
    for term in terms:
        size = rows // len(term)
        mine = []
        for i, part in enumerate(term):
            low, high = max(cut.start - i * size, 0), min(cut.stop - i * size, size)
            if low < high:
                used.append(part)
                mine.append(slice(low, high))
        cuts.append(mine)
    return pl.pallas_call(
        functools.partial(add_body, cuts),
        out_shape=jax.ShapeDtypeStruct((cut.stop - cut.start, used[0].shape[1]), BF16),
        in_specs=[full()] * len(used),
        out_specs=full(),
        cost_estimate=cost(0.3),
        compiler_params=pltpu.CompilerParams(vmem_limit_bytes=8 * 2**20),
        name="add",
    )(*used)


def shards(
    ring, resid, queries, span_kv, cache_kv, seg_len, o_rows, norm_gain, routes, route_wts, w_in, w_out
):
    count, pairs = ring.count, ring.pairs
    rows, width = queries.shape
    me = lax.axis_index("expert")
    lane = me % 2
    forward, backward, sibling = ring.step(1), ring.step(-1), ring.sibling()
    place = lax.axis_index("group") % 2 * count + me

    def ahead(block, name="rows out"):
        with jax.named_scope(name):
            return lax.ppermute(block, ("group", "expert"), forward)

    def across(block, name="to sibling"):
        with jax.named_scope(name):
            return lax.ppermute(block, "expert", sibling)

    group_swap = swap_pairs("group")
    groups = 4
    heads = HEADS // groups
    wide = heads * HD
    groups = 4
    heads = HEADS // groups
    slab = o_rows.shape[0]
    with jax.named_scope("far segment"):
        far = lax.ppermute(far_segment(seg_len, cache_kv), "group", group_swap)

    chain_a, other = pack(count, lane[None], o_rows, routes, route_wts)
    chain_b = across(other)
    blocks = [chain_a, chain_b]
    mine, theirs = [], []
    chains = [chain_a, chain_b]
    last = []

    def heads_of(j, held=None, after=()):
        part, *held = attend(j * heads, heads, queries, span_kv, cache_kv, far, seg_len, held, after)
        mine.append(part)
        theirs.append(across(part, f"attended {j}"))
        return held

    for s in range(1, pairs - HOPS_X):
        chains = [ahead(part, f"o rows {s}{'ab'[i]}") for i, part in enumerate(chains)]
        if s <= HOPS_X:
            with jax.named_scope("o rows of partner"):
                last.append([lax.ppermute(part, "group", group_swap) for part in chains])
        if s == HELD:
            (chains[0],) = heads_of(0, chains[0])
        blocks += chains
    if HELD == 0:
        heads_of(0)
    for j in range(1, groups):
        heads_of(j, after=last[AFTER[j]] if j in AFTER and AFTER[j] < len(last) else ())
    order = list(range(pairs - 1 - HOPS_X)) + list(range(pairs - HOPS_X, pairs)) + [pairs - 1 - HOPS_X]
    blocks, ends = blocks[:-2], blocks[-2:]
    for pair in reversed(last):
        blocks += pair
    blocks += ends
    tails = []
    with jax.named_scope("gate weights back"):
        tail = jnp.concatenate([blocks[0][slab:], blocks[1][slab:]], axis=0)
        for _ in range(HOPS_X):
            tail = lax.ppermute(tail, ("group", "expert"), backward)
            tails.insert(0, tail)
    sources = []
    for s in order:
        sources += [ring.source(s, 0), ring.source(s, 1)]
    table = jnp.asarray([[line[e] for line in sources] for e in range(2 * count)], jnp.int32)

    if slab != HD:
        mine, theirs = (
            [jnp.concatenate(p).transpose(1, 0, 2).reshape(rows, count, slab).transpose(1, 0, 2)]
            for p in (mine, theirs)
        )
    early = 2 * (pairs - 1 - HOPS_X)
    place = place[None]
    first_own, first_give, wts_early = project(table, place, 0, mine, theirs, [], blocks[:early], 0)
    own, give, wts_late = project(
        table, place, early, mine, theirs, [first_own, first_give], blocks[early:], 2, tails
    )
    got = across(give, "projected")
    residual, normed = norm(lane[None], resid, own, got, norm_gain)

    def gate_at(step, flip):
        column = 2 * order.index(step) + flip
        return (wts_early, column) if column < early else (wts_late, column - early)

    x, y = [normed], [across(normed, "normed")]

    def sums(s, after=()):
        wx, column_x = gate_at(s, 0)
        wy, column_y = gate_at((pairs - s) % pairs, 1)
        keep, give = expert((column_x, column_y), [x[s]], [y[s]], wx, wy, w_in, w_out, after)
        return keep, across(give, f"sums across {s}")

    def combine(terms, parts):
        terms = [term if isinstance(term, list) else [term] for term in terms if len(term)]
        return [
            add(slice(p * rows // parts, (p + 1) * rows // parts), rows, terms) for p in range(parts)
        ]

    travelling = []
    for s in range(1, pairs):
        x.append(ahead(x[-1], f"rows out {s}"))
        y.append(across(x[-1], f"rows across {s}"))
        keep, back = sums(s)
        total = combine([keep, back, travelling], 2 if s >= TAIL else 1)
        travelling = [ahead(part, f"sums out {s}{'ab'[i]}") for i, part in enumerate(total)]
    keep, back = sums(0, (x[min(3, pairs - 1)],))
    return combine([residual, keep, back, travelling], 1)[0]


def solution(mesh):
    placed = (
        P(("group", "expert"), None),
        P(("group", "expert"), None),
        P(None, ("group", "expert"), None),
        P(None, ("group", "expert"), None, None, None),
        P(("group", "expert"), None),
        P("expert", None),
        P(),
        P(("group", "expert"), None),
        P(("group", "expert"), None),
        P("expert", None, None),
        P("expert", None, None),
    )
    ring = Ring(mesh.shape["group"], mesh.shape["expert"])
    return jax.shard_map(
        functools.partial(shards, ring),
        mesh=mesh,
        in_specs=placed,
        out_specs=P(("group", "expert"), None),
        check_vma=False,
    )
```

```python
import functools
import math

import jax
import jax.numpy as jnp
from jax import lax
from jax.experimental import pallas as pl
from jax.experimental.pallas import tpu as pltpu
from jax.sharding import PartitionSpec as P

HEADS = 16
HD = 128
FF = 512
HOPS_X = 1
HELD = 4
AFTER = {3: 0}
TAIL = 5
DEAD = 128.0
ADD_COST = 2.0
EXPERT_COST = 4.0
AGP = 1
GIVE = 1
LATE = 3
FAR_MIB = 60
ATT_MIB = 8
PRO_MIB = 14
EXP_MIB = 16
SPEED = 6.0
F32 = jnp.float32
BF16 = jnp.bfloat16
SMEM = pltpu.SMEM


class Ring:
    def __init__(self, groups, count):
        self.groups, self.count = groups, count
        self.pairs = count // 2
        chips = list(range(0, self.pairs, 2)) + list(range(1, self.pairs, 2))[::-1]
        self.device = [[2 * c, 2 * c + 1] for c in chips]
        self.place = {self.device[i][k]: (i, k) for i in range(self.pairs) for k in (0, 1)}

    def at(self, i, k):
        return self.device[i % self.pairs][k]

    def way(self, g, k):
        return 1 if (g + k) % 2 == 0 else -1

    def step(self, sign):
        route = []
        for g in range(self.groups):
            for e, (i, k) in self.place.items():
                target = self.at(i + sign * self.way(g, k), k)
                route.append((g * self.count + e, g * self.count + target))
        return route

    def sibling(self):
        return [(e, e ^ 1) for e in range(self.count)]

    def source(self, s, flip_lane):
        out = []
        for g in (0, 1):
            for e in range(self.count):
                i, k = self.place[e]
                out.append(self.at(i - s * self.way(g, k), k ^ flip_lane))
        return out


def swap_pairs(axis):
    count = lax.axis_size(axis)
    route = []
    for low in range(0, count - 1, 2):
        route += [(low, low + 1), (low + 1, low)]
    return route


def attend_body(first, count, after, len_ref, q_ref, kv_ref, cache_ref, far_ref, *refs):
    out_ref = refs[after]
    rows = q_ref.shape[0]
    seg = far_ref.shape[1]
    dims = (((1,), (1,)), ((), ()))
    unit = (lax.broadcasted_iota(jnp.int32, (rows, HD), 1) == 0).astype(BF16)
    mark = lax.dot_general(unit, far_ref[0, :, :HD], dims, preferred_element_type=F32)
    near_ok = lax.broadcasted_iota(jnp.int32, (rows, seg), 1) < len_ref[0, 0]
    far_ok = mark < DEAD / 2
    scale = 1.0 / math.sqrt(HD)
    for h in range(count):
        cols = slice((first + h) * HD, (first + h + 1) * HD)
        q = q_ref[:, cols]
        s0 = lax.dot_general(q, kv_ref[0, :, cols], dims, preferred_element_type=F32) * scale
        s1 = lax.dot_general(q, cache_ref[0, 0, 0, :, cols], dims, preferred_element_type=F32) * scale
        s2 = lax.dot_general(q, far_ref[0, :, cols], dims, preferred_element_type=F32) * scale
        s1 = jnp.where(near_ok, s1, -1e30)
        s2 = jnp.where(far_ok, s2, -1e30)
        m = jnp.max(jnp.maximum(jnp.maximum(s0, s1), s2), axis=1, keepdims=True)
        w0 = jnp.exp(s0 - m)
        w1 = jnp.where(near_ok, jnp.exp(s1 - m), 0.0)
        w2 = jnp.where(far_ok, jnp.exp(s2 - m), 0.0)
        l = jnp.sum(w0 + w1 + w2, axis=1, keepdims=True)
        a = jnp.dot(w0.astype(BF16), kv_ref[1, :, cols], preferred_element_type=F32)
        a += jnp.dot(w1.astype(BF16), cache_ref[1, 0, 0, :, cols], preferred_element_type=F32)
        a += jnp.dot(w2.astype(BF16), far_ref[1, :, cols], preferred_element_type=F32)
        out_ref[h] = (a / l).astype(BF16)


def far_body(len_ref, cache_ref, out_ref, sems):
    copies = [pltpu.make_async_copy(cache_ref.at[i, 0, 1], out_ref.at[i], sems.at[i]) for i in (0, 1)]
    for copy in copies:
        copy.start()
    for copy in copies:
        copy.wait()
    row = lax.broadcasted_iota(jnp.int32, out_ref.shape[1:], 0)
    out_ref[0] = jnp.where(row < len_ref[0, 1], out_ref[0].astype(F32), DEAD).astype(BF16)


def far_segment(seg_len, cache_kv):
    return pl.pallas_call(
        far_body,
        out_shape=jax.ShapeDtypeStruct((2,) + cache_kv.shape[3:], BF16),
        in_specs=[scalars(), in_hbm()],
        out_specs=full(),
        scratch_shapes=[pltpu.SemaphoreType.DMA((2,))],
        cost_estimate=cost(1.7),
        compiler_params=pltpu.CompilerParams(vmem_limit_bytes=FAR_MIB * 2**20),
        name="far_segment",
    )(seg_len, cache_kv)


def cost(micros):
    return pl.CostEstimate(flops=int(micros * 1e9 * SPEED), bytes_accessed=1000, transcendentals=0)


def full():
    return pl.BlockSpec(memory_space=pltpu.VMEM)


def scalars():
    return pl.BlockSpec(memory_space=SMEM)


def in_hbm():
    return pl.BlockSpec(memory_space=pltpu.HBM)


def anywhere():
    return pl.BlockSpec(memory_space=pl.ANY)


def attend(first, count, queries, span_kv, cache_kv, far, seg_len, held=None, after=()):
    rows = queries.shape[0]
    out = [jax.ShapeDtypeStruct((count, rows, HD), BF16)]
    passed = [] if held is None else [held]
    out += [jax.ShapeDtypeStruct(p.shape, p.dtype) for p in passed]
    return pl.pallas_call(
        functools.partial(attend_body, first, count, len(passed) + len(after)),
        out_shape=out,
        in_specs=[scalars()] + [full()] * 4 + [anywhere()] * (len(passed) + len(after)),
        out_specs=[full()] + [anywhere()] * len(passed),
        input_output_aliases={5: 1} if passed else {},
        cost_estimate=cost(2.4),
        compiler_params=pltpu.CompilerParams(vmem_limit_bytes=ATT_MIB * 2**20),
        name="attend",
    )(seg_len, queries, span_kv, cache_kv, far, *passed, *after)


def pack_body(count, lane_ref, rows_ref, routes_ref, wts_ref, own_ref, other_ref):
    slab, half = rows_ref.shape[0], own_ref.shape[1]
    lane = lane_ref[0]
    own_ref[:slab] = rows_ref[:, pl.ds(pl.multiple_of(lane * half, HD), half)]
    other_ref[:slab] = rows_ref[:, pl.ds(pl.multiple_of((1 - lane) * half, HD), half)]
    routes = routes_ref[...]
    wts = wts_ref[...]
    tokens = wts.shape[1]
    high, low = [], []
    for group in range(count // 8):
        dense = jnp.concatenate(
            [
                jnp.sum(jnp.where(routes == group * 8 + j, wts, 0.0), axis=0, keepdims=True)
                for j in range(8)
            ],
            axis=0,
        )
        top = dense.astype(BF16)
        high.append(top)
        low.append((dense - top.astype(F32)).astype(BF16))
    tail = jnp.concatenate(high + low, axis=1)
    for out in (own_ref, other_ref):
        out[slab:, : tail.shape[1]] = tail
        if tail.shape[1] < half:
            out[slab:, tail.shape[1] :] = jnp.zeros((8, half - tail.shape[1]), BF16)


def pack(count, lane, o_rows, routes, route_wts):
    slab, width = o_rows.shape
    out = jax.ShapeDtypeStruct((slab + 8, width // 2), BF16)
    return pl.pallas_call(
        functools.partial(pack_body, count),
        out_shape=(out, out),
        in_specs=[scalars()] + [full()] * 3,
        out_specs=(full(), full()),
        cost_estimate=cost(0.7),
        compiler_params=pltpu.CompilerParams(vmem_limit_bytes=8 * 2**20),
        name="pack",
    )(lane, o_rows, routes.T, route_wts.T)


def project_body(first, blocks, pieces, carried, here, tail, table_ref, me_ref, *refs):
    refs = list(refs)
    mine = [refs.pop(0) for _ in range(pieces)]
    theirs = [refs.pop(0) for _ in range(pieces)]
    before = [refs.pop(0) for _ in range(2 if carried else 0)]
    source = [refs.pop(0) for _ in range(blocks)]
    tail_refs = [refs.pop(0) for _ in range(tail // 2)]
    own_ref, give_ref, wts_ref, att = refs[:4]
    rows = own_ref.shape[0]
    slab = att.shape[2]
    count = att.shape[0]
    copies = []
    if here < blocks:
        held, sems = refs[4:]
        away = range(blocks - here)
        copies = [pltpu.make_async_copy(source[b], held.at[b], sems.at[b]) for b in away]
        for copy in copies:
            copy.start()
        source = [held.at[b] for b in away] + source[blocks - here :]
    at = 0
    for a, b in zip(mine, theirs):
        att[at : at + a.shape[0], :rows] = a[...]
        att[at : at + a.shape[0], rows:] = b[...]
        at += a.shape[0]
    place = me_ref[0]
    me = lax.rem(place, count)
    sub, group = lax.rem(me, 8), me // 8
    groups = count // 8
    pick = lax.broadcasted_iota(jnp.int32, (8, rows), 0) == sub

    def line(ref, at):
        high = ref[at : at + 8, pl.ds(pl.multiple_of(group * rows, 128), rows)].astype(F32)
        low = ref[at : at + 8, pl.ds(pl.multiple_of((groups + group) * rows, 128), rows)].astype(F32)
        return jnp.sum(jnp.where(pick, high + low, 0.0), axis=0, keepdims=True)

    total = None
    lines = [None] * blocks
    for b in [*range(blocks - here, blocks), *range(blocks - here)]:
        if b < len(copies):
            copies[b].wait()
        head = att[table_ref[place, first + b]]
        part = jnp.dot(head, source[b][:slab], preferred_element_type=F32)
        total = part if total is None else total + part
        if b >= tail:
            lines[b] = line(source[b], slab)
    for i, ref in enumerate(tail_refs):
        lines[2 * i : 2 * i + 2] = [line(ref, 0), line(ref, 8)]
    if carried:
        own_ref[...] = before[0][...] + total[:rows]
        give_ref[...] = before[1][...] + total[rows:]
    else:
        own_ref[...] = total[:rows]
        give_ref[...] = total[rows:]
    lines.append(jnp.zeros((128 - blocks, rows), F32))
    wts_ref[...] = jnp.concatenate(lines, axis=0).T


def project(table, place, first, mine, theirs, before, blocks, here, tails=()):
    count = sum(part.shape[0] for part in mine)
    rows, slab = mine[0].shape[1:]
    half = blocks[0].shape[1]
    out = jax.ShapeDtypeStruct((rows, half), F32)
    number = len(blocks)
    scratch = [pltpu.VMEM((count, 2 * rows, slab), BF16)]
    away = number - here
    if away:
        scratch += [pltpu.VMEM((away,) + blocks[0].shape, BF16), pltpu.SemaphoreType.DMA((away,))]
    return pl.pallas_call(
        functools.partial(
            project_body, first, number, len(mine), bool(before), here, 2 * len(tails)
        ),
        out_shape=(out, out, jax.ShapeDtypeStruct((rows, 128), F32)),
        in_specs=[scalars(), scalars()]
        + [full()] * (2 * len(mine) + len(before))
        + [in_hbm()] * away
        + [full()] * here
        + [full()] * len(tails),
        out_specs=(full(), full(), full()),
        scratch_shapes=scratch,
        cost_estimate=pl.CostEstimate(
            flops=4 * rows * half * slab * number, bytes_accessed=2 * half * slab * number, transcendentals=0
        ),
        compiler_params=pltpu.CompilerParams(vmem_limit_bytes=PRO_MIB * 2**20),
        name="project",
    )(table, place, *mine, *theirs, *before, *blocks, *tails)


def norm_body(lane_ref, resid_ref, own_ref, got_ref, gain_ref, sum_ref, out_ref):
    first = lane_ref[0] == 0
    half = own_ref.shape[1]
    own = own_ref[...]
    got = got_ref[...]
    low = resid_ref[:, :half].astype(F32) + jnp.where(first, own, got)
    high = resid_ref[:, half:].astype(F32) + jnp.where(first, got, own)
    sum_ref[:, :half] = low
    sum_ref[:, half:] = high
    square = jnp.sum(low * low + high * high, axis=1, keepdims=True)
    scale = lax.rsqrt(square * (1.0 / (2 * half)) + 1e-05)
    out_ref[:, :half] = (low * scale * gain_ref[:, :half]).astype(BF16)
    out_ref[:, half:] = (high * scale * gain_ref[:, half:]).astype(BF16)


def norm(lane, resid, own, got, gain):
    return pl.pallas_call(
        norm_body,
        out_shape=(
            jax.ShapeDtypeStruct(resid.shape, F32),
            jax.ShapeDtypeStruct(resid.shape, BF16),
        ),
        in_specs=[scalars()] + [full()] * 4,
        out_specs=(full(), full()),
        cost_estimate=cost(0.4),
        compiler_params=pltpu.CompilerParams(vmem_limit_bytes=16 * 2**20),
        name="norm",
    )(lane, resid, own, got, gain.reshape(1, -1))


def expert_body(cols, parts, after, gives, *refs):
    refs = list(refs)
    xy, (wx_ref, wy_ref, in_ref, down_ref) = refs[: 2 * parts], refs[2 * parts : 2 * parts + 4]
    cx_ref, *cy_refs = refs[2 * parts + 4 + after :]
    rows, width = cx_ref.shape
    size = rows // gives
    both = jnp.concatenate([ref[...] for ref in xy], axis=0)
    gate = jnp.dot(both, in_ref[0, :, :FF], preferred_element_type=F32)
    up = jnp.dot(both, in_ref[0, :, FF:], preferred_element_type=F32)
    hidden = (gate * jax.nn.sigmoid(gate) * up).astype(BF16)
    wx = wx_ref[:, cols[0] : cols[0] + 1]
    wy = wy_ref[:, cols[1] : cols[1] + 1]
    step = 512
    for at in range(0, width, step):
        out = jnp.dot(hidden, down_ref[0, :, at : at + step], preferred_element_type=F32)
        cx_ref[:, at : at + step] = (out[:rows] * wx).astype(BF16)
        cy = (out[rows:] * wy).astype(BF16)
        for i, cy_ref in enumerate(cy_refs):
            cy_ref[:, at : at + step] = cy[i * size : (i + 1) * size]


def expert(cols, x, y, wx, wy, w_in, w_out, after=(), gives=1):
    rows, width = wx.shape[0], w_out.shape[2]
    parts = len(x)
    out = jax.ShapeDtypeStruct((rows, width), BF16)
    part = jax.ShapeDtypeStruct((rows // gives, width), BF16)
    return pl.pallas_call(
        functools.partial(expert_body, cols, parts, len(after), gives),
        out_shape=(out,) + (part,) * gives,
        in_specs=[full()] * (2 * parts + 4) + [anywhere()] * len(after),
        out_specs=(full(),) * (1 + gives),
        cost_estimate=cost(EXPERT_COST),
        compiler_params=pltpu.CompilerParams(vmem_limit_bytes=EXP_MIB * 2**20),
        name="expert",
    )(*x, *y, wx, wy, w_in, w_out, *after)


def add_body(cuts, *refs):
    total = None
    at = 0
    for cut in cuts:
        term = jnp.concatenate([ref[c].astype(F32) for ref, c in zip(refs[at:], cut)], axis=0)
        at += len(cut)
        total = term if total is None else total + term
    refs[-1][...] = total.astype(BF16)


def add(cut, rows, terms):
    used, cuts = [], []
    for term in terms:
        size = rows // len(term)
        mine = []
        for i, part in enumerate(term):
            low, high = max(cut.start - i * size, 0), min(cut.stop - i * size, size)
            if low < high:
                used.append(part)
                mine.append(slice(low, high))
        cuts.append(mine)
    return pl.pallas_call(
        functools.partial(add_body, cuts),
        out_shape=jax.ShapeDtypeStruct((cut.stop - cut.start, used[0].shape[1]), BF16),
        in_specs=[full()] * len(used),
        out_specs=full(),
        cost_estimate=cost(ADD_COST),
        compiler_params=pltpu.CompilerParams(vmem_limit_bytes=8 * 2**20),
        name="add",
    )(*used)


def shards(
    ring, resid, queries, span_kv, cache_kv, seg_len, o_rows, norm_gain, routes, route_wts, w_in, w_out
):
    count, pairs = ring.count, ring.pairs
    rows, width = queries.shape
    me = lax.axis_index("expert")
    lane = me % 2
    forward, backward, sibling = ring.step(1), ring.step(-1), ring.sibling()
    place = lax.axis_index("group") % 2 * count + me

    def ahead(block, name="rows out"):
        with jax.named_scope(name):
            return lax.ppermute(block, ("group", "expert"), forward)

    def across(block, name="to sibling"):
        with jax.named_scope(name):
            return lax.ppermute(block, "expert", sibling)

    group_swap = swap_pairs("group")
    groups = 4
    heads = HEADS // groups
    wide = heads * HD
    groups = 4
    heads = HEADS // groups
    slab = o_rows.shape[0]
    with jax.named_scope("far segment"):
        far = lax.ppermute(far_segment(seg_len, cache_kv), "group", group_swap)

    chain_a, other = pack(count, lane[None], o_rows, routes, route_wts)
    chain_b = across(other)
    blocks = [chain_a, chain_b]
    mine, theirs = [], []
    chains = [chain_a, chain_b]
    last = []

    def heads_of(j, held=None, after=()):
        part, *held = attend(j * heads, heads, queries, span_kv, cache_kv, far, seg_len, held, after)
        mine.append(part)
        theirs.append(across(part, f"attended {j}"))
        return held

    for s in range(1, pairs - HOPS_X):
        chains = [ahead(part, f"o rows {s}{'ab'[i]}") for i, part in enumerate(chains)]
        if s <= HOPS_X:
            with jax.named_scope("o rows of partner"):
                last.append([lax.ppermute(part, "group", group_swap) for part in chains])
        if s == HELD:
            (chains[0],) = heads_of(0, chains[0])
        blocks += chains
    if HELD == 0:
        heads_of(0)
    for j in range(1, groups):
        heads_of(j, after=last[AFTER[j]] if j in AFTER and AFTER[j] < len(last) else ())
    order = list(range(pairs - 1 - HOPS_X)) + list(range(pairs - HOPS_X, pairs)) + [pairs - 1 - HOPS_X]
    blocks, ends = blocks[:-2], blocks[-2:]
    for pair in reversed(last):
        blocks += pair
    blocks += ends
    tails = []
    with jax.named_scope("gate weights back"):
        tail = jnp.concatenate([blocks[0][slab:], blocks[1][slab:]], axis=0)
        for _ in range(HOPS_X):
            tail = lax.ppermute(tail, ("group", "expert"), backward)
            tails.insert(0, tail)
    sources = []
    for s in order:
        sources += [ring.source(s, 0), ring.source(s, 1)]
    table = jnp.asarray([[line[e] for line in sources] for e in range(2 * count)], jnp.int32)

    if slab != HD:
        mine, theirs = (
            [jnp.concatenate(p).transpose(1, 0, 2).reshape(rows, count, slab).transpose(1, 0, 2)]
            for p in (mine, theirs)
        )
    early = 2 * (pairs - 1 - HOPS_X)
    place = place[None]
    first_own, first_give, wts_early = project(table, place, 0, mine, theirs, [], blocks[:early], 0)
    own, give, wts_late = project(
        table, place, early, mine, theirs, [first_own, first_give], blocks[early:], 2, tails
    )
    got = across(give, "projected")
    residual, normed = norm(lane[None], resid, own, got, norm_gain)

    def gate_at(step, flip):
        column = 2 * order.index(step) + flip
        return (wts_early, column) if column < early else (wts_late, column - early)

    size = rows // AGP
    x = [[normed[p * size : (p + 1) * size] for p in range(AGP)]]
    y = [[across(part, "normed") for part in x[0]]]

    def sums(s, after=()):
        wx, column_x = gate_at(s, 0)
        wy, column_y = gate_at((pairs - s) % pairs, 1)
        keep, *give = expert((column_x, column_y), x[s], y[s], wx, wy, w_in, w_out, after, GIVE)
        return keep, [across(part, f"sums across {s}{'ab'[i]}") for i, part in enumerate(give)]

    def combine(terms, parts):
        terms = [term if isinstance(term, list) else [term] for term in terms if len(term)]
        return [
            add(slice(p * rows // parts, (p + 1) * rows // parts), rows, terms) for p in range(parts)
        ]

    travelling = []
    for s in range(1, pairs):
        x.append([ahead(part, f"rows out {s}{'ab'[i]}") for i, part in enumerate(x[-1])])
        y.append([across(part, f"rows across {s}{'ab'[i]}") for i, part in enumerate(x[-1])])
        keep, back = sums(s)
        total = combine([keep, back, travelling], 2 if s >= TAIL else 1)
        travelling = [ahead(part, f"sums out {s}{'ab'[i]}") for i, part in enumerate(total)]
    keep, back = sums(0, (x[min(LATE, pairs - 1)][0],))
    return combine([residual, keep, back, travelling], 1)[0]


def solution(mesh):
    placed = (
        P(("group", "expert"), None),
        P(("group", "expert"), None),
        P(None, ("group", "expert"), None),
        P(None, ("group", "expert"), None, None, None),
        P(("group", "expert"), None),
        P("expert", None),
        P(),
        P(("group", "expert"), None),
        P(("group", "expert"), None),
        P("expert", None, None),
        P("expert", None, None),
    )
    ring = Ring(mesh.shape["group"], mesh.shape["expert"])
    return jax.shard_map(
        functools.partial(shards, ring),
        mesh=mesh,
        in_specs=placed,
        out_specs=P(("group", "expert"), None),
        check_vma=False,
    )
```

```python
import functools
import math

import jax
import jax.numpy as jnp
from jax import lax
from jax.experimental import pallas as pl
from jax.experimental.pallas import tpu as pltpu
from jax.sharding import PartitionSpec as P

HEADS = 16
HD = 128
FF = 512
HOPS_X = 1
HELD = 4
AFTER = {3: 0}
TAIL = 5
DEAD = 128.0
ADD_COST = 2.0
EXPERT_COST = 4.0
AGP = 1
GIVE = 1
LATE = 3
FAR_MIB = 60
ATT_MIB = 8
PRO_MIB = 14
EXP_MIB = 16
SPEED = 6.0
F32 = jnp.float32
BF16 = jnp.bfloat16
SMEM = pltpu.SMEM


class Ring:
    def __init__(self, groups, count):
        self.groups, self.count = groups, count
        self.pairs = count // 2
        chips = list(range(0, self.pairs, 2)) + list(range(1, self.pairs, 2))[::-1]
        self.device = [[2 * c, 2 * c + 1] for c in chips]
        self.place = {self.device[i][k]: (i, k) for i in range(self.pairs) for k in (0, 1)}

    def at(self, i, k):
        return self.device[i % self.pairs][k]

    def way(self, g, k):
        return 1 if (g + k) % 2 == 0 else -1

    def step(self):
        return [
            (g * self.count + e, g * self.count + self.at(i + self.way(g, k), k))
            for g in range(self.groups)
            for e, (i, k) in self.place.items()
        ]

    def back(self, flip_lane):
        return [
            (g * self.count + self.at(i + self.way(g, k), k ^ flip_lane), g * self.count + e)
            for g in range(self.groups)
            for e, (i, k) in self.place.items()
        ]

    def sibling(self):
        return [(e, e ^ 1) for e in range(self.count)]

    def source(self, place, s, flip_lane):
        me, odd = lax.rem(place, self.count), place // self.count
        chip, lane = me // 2, lax.rem(me, 2)
        evens = (self.pairs + 1) // 2
        i = jnp.where(lax.rem(chip, 2) == 0, chip // 2, self.pairs - 1 - chip // 2)
        way = 1 - 2 * lax.rem(odd + lane, 2)
        i = lax.rem(i - s * way + 2 * self.pairs, self.pairs)
        chip = jnp.where(i < evens, 2 * i, 2 * (self.pairs - 1 - i) + 1)
        return 2 * chip + lax.rem(lane + flip_lane, 2)


def swap_pairs(axis):
    count = lax.axis_size(axis)
    route = []
    for low in range(0, count - 1, 2):
        route += [(low, low + 1), (low + 1, low)]
    return route


def attend_body(first, count, after, len_ref, q_ref, kv_ref, cache_ref, far_ref, *refs):
    out_ref = refs[after]
    rows = q_ref.shape[0]
    seg = far_ref.shape[1]
    dims = (((1,), (1,)), ((), ()))
    unit = (lax.broadcasted_iota(jnp.int32, (rows, HD), 1) == 0).astype(BF16)
    mark = lax.dot_general(unit, far_ref[0, :, :HD], dims, preferred_element_type=F32)
    near_ok = lax.broadcasted_iota(jnp.int32, (rows, seg), 1) < len_ref[0, 0]
    far_ok = mark < DEAD / 2
    scale = 1.0 / math.sqrt(HD)
    for h in range(count):
        cols = slice((first + h) * HD, (first + h + 1) * HD)
        own = slice(h * HD, (h + 1) * HD)
        q = q_ref[:, cols]
        s0 = lax.dot_general(q, kv_ref[0, :, cols], dims, preferred_element_type=F32) * scale
        s1 = lax.dot_general(q, cache_ref[0, 0, 0, :, cols], dims, preferred_element_type=F32) * scale
        s2 = lax.dot_general(q, far_ref[0, :, own], dims, preferred_element_type=F32) * scale
        s1 = jnp.where(near_ok, s1, -1e30)
        s2 = jnp.where(far_ok, s2, -1e30)
        m = jnp.max(jnp.maximum(jnp.maximum(s0, s1), s2), axis=1, keepdims=True)
        w0 = jnp.exp(s0 - m)
        w1 = jnp.where(near_ok, jnp.exp(s1 - m), 0.0)
        w2 = jnp.where(far_ok, jnp.exp(s2 - m), 0.0)
        l = jnp.sum(w0 + w1 + w2, axis=1, keepdims=True)
        a = jnp.dot(w0.astype(BF16), kv_ref[1, :, cols], preferred_element_type=F32)
        a += jnp.dot(w1.astype(BF16), cache_ref[1, 0, 0, :, cols], preferred_element_type=F32)
        a += jnp.dot(w2.astype(BF16), far_ref[1, :, own], preferred_element_type=F32)
        out_ref[h] = (a / l).astype(BF16)


def far_body(len_ref, cache_ref, out_ref, sems):
    copies = [pltpu.make_async_copy(cache_ref.at[i, 0, 1], out_ref.at[i], sems.at[i]) for i in (0, 1)]
    for copy in copies:
        copy.start()
    for copy in copies:
        copy.wait()
    row = lax.broadcasted_iota(jnp.int32, out_ref.shape[1:], 0)
    out_ref[0] = jnp.where(row < len_ref[0, 1], out_ref[0].astype(F32), DEAD).astype(BF16)


def far_segment(seg_len, cache_kv):
    return pl.pallas_call(
        far_body,
        out_shape=jax.ShapeDtypeStruct((2,) + cache_kv.shape[3:], BF16),
        in_specs=[scalars(), in_hbm()],
        out_specs=full(),
        scratch_shapes=[pltpu.SemaphoreType.DMA((2,))],
        cost_estimate=cost(1.7),
        compiler_params=pltpu.CompilerParams(vmem_limit_bytes=FAR_MIB * 2**20),
        name="far_segment",
    )(seg_len, cache_kv)


def cost(micros):
    return pl.CostEstimate(flops=int(micros * 1e9 * SPEED), bytes_accessed=1000, transcendentals=0)


def full():
    return pl.BlockSpec(memory_space=pltpu.VMEM)


def scalars():
    return pl.BlockSpec(memory_space=SMEM)


def in_hbm():
    return pl.BlockSpec(memory_space=pltpu.HBM)


def anywhere():
    return pl.BlockSpec(memory_space=pl.ANY)


def attend(first, count, queries, span_kv, cache_kv, far, seg_len, held=None, after=()):
    rows = queries.shape[0]
    out = [jax.ShapeDtypeStruct((count, rows, HD), BF16)]
    passed = [] if held is None else [held]
    out += [jax.ShapeDtypeStruct(p.shape, p.dtype) for p in passed]
    return pl.pallas_call(
        functools.partial(attend_body, first, count, len(passed) + len(after)),
        out_shape=out,
        grid=(1,),
        in_specs=[scalars()]
        + [full()] * 3
        + [pl.BlockSpec((2, far.shape[1], count * HD), lambda i: (0, 0, first // count))]
        + [anywhere()] * (len(passed) + len(after)),
        out_specs=[full()] + [anywhere()] * len(passed),
        input_output_aliases={5: 1} if passed else {},
        cost_estimate=cost(2.4),
        compiler_params=pltpu.CompilerParams(vmem_limit_bytes=ATT_MIB * 2**20),
        name="attend",
    )(seg_len, queries, span_kv, cache_kv, far, *passed, *after)


def pack_body(count, lane_ref, rows_ref, routes_ref, wts_ref, own_ref, other_ref, tail_ref):
    slab, half = rows_ref.shape[0], own_ref.shape[1]
    lane = lane_ref[0]
    own_ref[:slab] = rows_ref[:, pl.ds(pl.multiple_of(lane * half, HD), half)]
    other_ref[:slab] = rows_ref[:, pl.ds(pl.multiple_of((1 - lane) * half, HD), half)]
    routes = routes_ref[...]
    wts = wts_ref[...]
    tokens = wts.shape[1]
    high, low = [], []
    for group in range(count // 8):
        dense = jnp.concatenate(
            [
                jnp.sum(jnp.where(routes == group * 8 + j, wts, 0.0), axis=0, keepdims=True)
                for j in range(8)
            ],
            axis=0,
        )
        top = dense.astype(BF16)
        high.append(top)
        low.append((dense - top.astype(F32)).astype(BF16))
    tail = jnp.concatenate(high + low, axis=1)
    for out in (own_ref, other_ref):
        out[slab:, : tail.shape[1]] = tail
        if tail.shape[1] < half:
            out[slab:, tail.shape[1] :] = jnp.zeros((8, half - tail.shape[1]), BF16)
    tail_ref[:8, : tail.shape[1]] = tail
    tail_ref[8:, : tail.shape[1]] = jnp.zeros_like(tail)
    if tail.shape[1] < half:
        tail_ref[:, tail.shape[1] :] = jnp.zeros((16, half - tail.shape[1]), BF16)


def pack(count, lane, o_rows, routes, route_wts):
    slab, width = o_rows.shape
    out = jax.ShapeDtypeStruct((slab + 8, width // 2), BF16)
    return pl.pallas_call(
        functools.partial(pack_body, count),
        out_shape=(out, out, jax.ShapeDtypeStruct((16, width // 2), BF16)),
        in_specs=[scalars()] + [full()] * 3,
        out_specs=(full(), full(), full()),
        cost_estimate=cost(0.7),
        compiler_params=pltpu.CompilerParams(vmem_limit_bytes=8 * 2**20),
        name="pack",
    )(lane, o_rows, routes.T, route_wts.T)


def project_body(ring, steps, blocks, pieces, carried, here, tail, me_ref, *refs):
    refs = list(refs)
    mine = [refs.pop(0) for _ in range(pieces)]
    theirs = [refs.pop(0) for _ in range(pieces)]
    before = [refs.pop(0) for _ in range(2 if carried else 0)]
    source = [refs.pop(0) for _ in range(blocks)]
    tail_refs = [refs.pop(0) for _ in range(tail)]
    own_ref, give_ref, wts_ref, att = refs[:4]
    rows = own_ref.shape[0]
    slab = att.shape[2]
    count = att.shape[0]
    copies = []
    if here < blocks:
        held, sems = refs[4:]
        away = range(blocks - here)
        copies = [pltpu.make_async_copy(source[b], held.at[b], sems.at[b]) for b in away]
        for copy in copies:
            copy.start()
        source = [held.at[b] for b in away] + source[blocks - here :]
    at = 0
    for a, b in zip(mine, theirs):
        att[at : at + a.shape[0], :rows] = a[...]
        att[at : at + a.shape[0], rows:] = b[...]
        at += a.shape[0]
    place = me_ref[0]
    me = lax.rem(place, count)
    sub, group = lax.rem(me, 8), me // 8
    groups = count // 8
    pick = lax.broadcasted_iota(jnp.int32, (8, rows), 0) == sub

    def line(ref, at):
        high = ref[at : at + 8, pl.ds(pl.multiple_of(group * rows, 128), rows)].astype(F32)
        low = ref[at : at + 8, pl.ds(pl.multiple_of((groups + group) * rows, 128), rows)].astype(F32)
        return jnp.sum(jnp.where(pick, high + low, 0.0), axis=0, keepdims=True)

    total = None
    lines = [None] * blocks
    for b in [*range(blocks - here, blocks), *range(blocks - here)]:
        if b < len(copies):
            copies[b].wait()
        head = att[ring.source(place, steps[b // 2], b % 2)]
        part = jnp.dot(head, source[b][:slab], preferred_element_type=F32)
        total = part if total is None else total + part
        if b >= tail:
            lines[b] = line(source[b], slab)
    for i, ref in enumerate(tail_refs):
        lines[i] = line(ref, 0)
    if carried:
        own_ref[...] = before[0][...] + total[:rows]
        give_ref[...] = (before[1][...] + total[rows:]).astype(give_ref.dtype)
    else:
        own_ref[...] = total[:rows]
        give_ref[...] = total[rows:]
    lines.append(jnp.zeros((128 - blocks, rows), F32))
    wts_ref[...] = jnp.concatenate(lines, axis=0).T


def project(ring, place, steps, mine, theirs, before, blocks, here, tails=()):
    count = sum(part.shape[0] for part in mine)
    rows, slab = mine[0].shape[1:]
    half = blocks[0].shape[1]
    out = jax.ShapeDtypeStruct((rows, half), F32)
    number = len(blocks)
    scratch = [pltpu.VMEM((count, 2 * rows, slab), BF16)]
    away = number - here
    if away:
        scratch += [pltpu.VMEM((away,) + blocks[0].shape, BF16), pltpu.SemaphoreType.DMA((away,))]
    return pl.pallas_call(
        functools.partial(
            project_body, ring, steps, number, len(mine), bool(before), here, len(tails)
        ),
        out_shape=(
            out,
            jax.ShapeDtypeStruct((rows, half), BF16 if before else F32),
            jax.ShapeDtypeStruct((rows, 128), F32),
        ),
        in_specs=[scalars()]
        + [full()] * (2 * len(mine) + len(before))
        + [in_hbm()] * away
        + [full()] * here
        + [full()] * len(tails),
        out_specs=(full(), full(), full()),
        scratch_shapes=scratch,
        cost_estimate=pl.CostEstimate(
            flops=4 * rows * half * slab * number, bytes_accessed=2 * half * slab * number, transcendentals=0
        ),
        compiler_params=pltpu.CompilerParams(vmem_limit_bytes=PRO_MIB * 2**20),
        name="project",
    )(place, *mine, *theirs, *before, *blocks, *tails)


def norm_body(lane_ref, resid_ref, own_ref, got_ref, gain_ref, sum_ref, out_ref):
    first = lane_ref[0] == 0
    half = own_ref.shape[1]
    own = own_ref[...]
    got = got_ref[...].astype(F32)
    low = resid_ref[:, :half].astype(F32) + jnp.where(first, own, got)
    high = resid_ref[:, half:].astype(F32) + jnp.where(first, got, own)
    sum_ref[:, :half] = low
    sum_ref[:, half:] = high
    square = jnp.sum(low * low + high * high, axis=1, keepdims=True)
    scale = lax.rsqrt(square * (1.0 / (2 * half)) + 1e-05)
    out_ref[:, :half] = (low * scale * gain_ref[:, :half]).astype(BF16)
    out_ref[:, half:] = (high * scale * gain_ref[:, half:]).astype(BF16)


def norm(lane, resid, own, got, gain):
    return pl.pallas_call(
        norm_body,
        out_shape=(
            jax.ShapeDtypeStruct(resid.shape, F32),
            jax.ShapeDtypeStruct(resid.shape, BF16),
        ),
        in_specs=[scalars()] + [full()] * 4,
        out_specs=(full(), full()),
        cost_estimate=cost(0.4),
        compiler_params=pltpu.CompilerParams(vmem_limit_bytes=16 * 2**20),
        name="norm",
    )(lane, resid, own, got, gain.reshape(1, -1))


def expert_body(cols, parts, after, gives, *refs):
    refs = list(refs)
    xy, (wx_ref, wy_ref, in_ref, down_ref) = refs[: 2 * parts], refs[2 * parts : 2 * parts + 4]
    cx_ref, *cy_refs = refs[2 * parts + 4 + after :]
    rows, width = cx_ref.shape
    size = rows // gives
    both = jnp.concatenate([ref[...] for ref in xy], axis=0)
    gate = jnp.dot(both, in_ref[0, :, :FF], preferred_element_type=F32)
    up = jnp.dot(both, in_ref[0, :, FF:], preferred_element_type=F32)
    hidden = (gate * jax.nn.sigmoid(gate) * up).astype(BF16)
    wx = wx_ref[:, cols[0] : cols[0] + 1]
    wy = wy_ref[:, cols[1] : cols[1] + 1]
    step = 512
    for at in range(0, width, step):
        out = jnp.dot(hidden, down_ref[0, :, at : at + step], preferred_element_type=F32)
        cx_ref[:, at : at + step] = (out[:rows] * wx).astype(BF16)
        cy = (out[rows:] * wy).astype(BF16)
        for i, cy_ref in enumerate(cy_refs):
            cy_ref[:, at : at + step] = cy[i * size : (i + 1) * size]


def expert(cols, x, y, wx, wy, w_in, w_out, after=(), gives=1):
    rows, width = wx.shape[0], w_out.shape[2]
    parts = len(x)
    out = jax.ShapeDtypeStruct((rows, width), BF16)
    part = jax.ShapeDtypeStruct((rows // gives, width), BF16)
    return pl.pallas_call(
        functools.partial(expert_body, cols, parts, len(after), gives),
        out_shape=(out,) + (part,) * gives,
        in_specs=[full()] * (2 * parts + 4) + [anywhere()] * len(after),
        out_specs=(full(),) * (1 + gives),
        cost_estimate=cost(EXPERT_COST),
        compiler_params=pltpu.CompilerParams(vmem_limit_bytes=EXP_MIB * 2**20),
        name="expert",
    )(*x, *y, wx, wy, w_in, w_out, *after)


def add_body(cuts, *refs):
    total = None
    at = 0
    for cut in cuts:
        term = jnp.concatenate([ref[c].astype(F32) for ref, c in zip(refs[at:], cut)], axis=0)
        at += len(cut)
        total = term if total is None else total + term
    refs[-1][...] = total.astype(refs[-1].dtype)


def add(cut, rows, terms, kind):
    used, cuts = [], []
    for term in terms:
        size = rows // len(term)
        mine = []
        for i, part in enumerate(term):
            low, high = max(cut.start - i * size, 0), min(cut.stop - i * size, size)
            if low < high:
                used.append(part)
                mine.append(slice(low, high))
        cuts.append(mine)
    return pl.pallas_call(
        functools.partial(add_body, cuts),
        out_shape=jax.ShapeDtypeStruct((cut.stop - cut.start, used[0].shape[1]), kind),
        in_specs=[full()] * len(used),
        out_specs=full(),
        cost_estimate=cost(ADD_COST),
        compiler_params=pltpu.CompilerParams(vmem_limit_bytes=8 * 2**20),
        name="add",
    )(*used)


def shards(
    ring, resid, queries, span_kv, cache_kv, seg_len, o_rows, norm_gain, routes, route_wts, w_in, w_out
):
    count, pairs = ring.count, ring.pairs
    rows, width = queries.shape
    me = lax.axis_index("expert")
    lane = me % 2
    forward, sibling = ring.step(), ring.sibling()
    place = lax.axis_index("group") % 2 * count + me

    def ahead(block, name="rows out"):
        with jax.named_scope(name):
            return lax.ppermute(block, ("group", "expert"), forward)

    def across(block, name="to sibling"):
        with jax.named_scope(name):
            return lax.ppermute(block, "expert", sibling)

    group_swap = swap_pairs("group")
    groups = 4
    heads = HEADS // groups
    wide = heads * HD
    groups = 4
    heads = HEADS // groups
    slab = o_rows.shape[0]
    with jax.named_scope("far segment"):
        far = lax.ppermute(far_segment(seg_len, cache_kv), "group", group_swap)

    chain_a, other, tail = pack(count, lane[None], o_rows, routes, route_wts)
    chain_b = across(other)
    blocks = [chain_a, chain_b]
    mine, theirs = [], []
    chains = [chain_a, chain_b]
    last = []

    def heads_of(j, held=None, after=()):
        part, *held = attend(j * heads, heads, queries, span_kv, cache_kv, far, seg_len, held, after)
        mine.append(part)
        theirs.append(across(part, f"attended {j}"))
        return held

    for s in range(1, pairs - HOPS_X):
        chains = [ahead(part, f"o rows {s}{'ab'[i]}") for i, part in enumerate(chains)]
        if s <= HOPS_X:
            with jax.named_scope("o rows of partner"):
                last.append([lax.ppermute(part, "group", group_swap) for part in chains])
        if s == HELD:
            (chains[0],) = heads_of(0, chains[0])
        blocks += chains
    if HELD == 0:
        heads_of(0)
    for j in range(1, groups):
        heads_of(j, after=last[AFTER[j]] if j in AFTER and AFTER[j] < len(last) else ())
    order = list(range(pairs - 1 - HOPS_X)) + list(range(pairs - HOPS_X, pairs)) + [pairs - 1 - HOPS_X]
    blocks, ends = blocks[:-2], blocks[-2:]
    for pair in reversed(last):
        blocks += pair
    blocks += ends
    tails = []
    with jax.named_scope("gate weights back"):
        for route in (ring.back(0), ring.back(1)) if HOPS_X else ():
            tails.append(lax.ppermute(tail, ("group", "expert"), route))
    if slab != HD:
        mine, theirs = (
            [jnp.concatenate(p).transpose(1, 0, 2).reshape(rows, count, slab).transpose(1, 0, 2)]
            for p in (mine, theirs)
        )
    early = 2 * (pairs - 1 - HOPS_X)
    place = place[None]
    first_own, first_give, wts_early = project(ring, place, order[: early // 2], mine, theirs, [], blocks[:early], 0)
    own, give, wts_late = project(
        ring, place, order[early // 2 :], mine, theirs, [first_own, first_give], blocks[early:], 2, tails
    )
    got = across(give, "projected")
    residual, normed = norm(lane[None], resid, own, got, norm_gain)

    def gate_at(step, flip):
        column = 2 * order.index(step) + flip
        return (wts_early, column) if column < early else (wts_late, column - early)

    size = rows // AGP
    x = [[normed[p * size : (p + 1) * size] for p in range(AGP)]]
    y = [[across(part, "normed") for part in x[0]]]

    def sums(s, after=()):
        wx, column_x = gate_at(s, 0)
        wy, column_y = gate_at((pairs - s) % pairs, 1)
        keep, *give = expert((column_x, column_y), x[s], y[s], wx, wy, w_in, w_out, after, GIVE)
        return keep, [across(part, f"sums across {s}{'ab'[i]}") for i, part in enumerate(give)]

    def combine(terms, parts, kind=BF16):
        terms = [term if isinstance(term, list) else [term] for term in terms if len(term)]
        return [
            add(slice(p * rows // parts, (p + 1) * rows // parts), rows, terms, kind) for p in range(parts)
        ]

    travelling = []
    for s in range(1, pairs):
        x.append([ahead(part, f"rows out {s}{'ab'[i]}") for i, part in enumerate(x[-1])])
        y.append([across(part, f"rows across {s}{'ab'[i]}") for i, part in enumerate(x[-1])])
        keep, back = sums(s)
        total = combine([keep, back, travelling], 2 if s >= TAIL else 1)
        travelling = [ahead(part, f"sums out {s}{'ab'[i]}") for i, part in enumerate(total)]
    base = combine([residual, *sums(0, (x[min(LATE, pairs - 1)][0],))], 1, F32)
    return combine([base, travelling], 1)[0]


def solution(mesh):
    placed = (
        P(("group", "expert"), None),
        P(("group", "expert"), None),
        P(None, ("group", "expert"), None),
        P(None, ("group", "expert"), None, None, None),
        P(("group", "expert"), None),
        P("expert", None),
        P(),
        P(("group", "expert"), None),
        P(("group", "expert"), None),
        P("expert", None, None),
        P("expert", None, None),
    )
    ring = Ring(mesh.shape["group"], mesh.shape["expert"])
    return jax.shard_map(
        functools.partial(shards, ring),
        mesh=mesh,
        in_specs=placed,
        out_specs=P(("group", "expert"), None),
        check_vma=False,
    )
```

```python
import functools
import math

import jax
import jax.numpy as jnp
from jax import lax
from jax.experimental import pallas as pl
from jax.experimental.pallas import tpu as pltpu
from jax.sharding import PartitionSpec as P

HEADS = 16
HD = 128
FF = 512
HOPS_X = 1
HELD = 4
AFTER = {3: 0}
HALVED = (5, 6, 7)
DEAD = 128.0
ADD_COST = 2.0
EXPERT_COST = 4.0
AGP = 1
GIVE = 1
LATE = 2
FAR_MIB = 60
ATT_MIB = 8
PRO_MIB = 14
EXP_MIB = 16
SPEED = 6.0
F32 = jnp.float32
BF16 = jnp.bfloat16
SMEM = pltpu.SMEM


class Ring:
    def __init__(self, groups, count):
        self.groups, self.count = groups, count
        self.pairs = count // 2
        chips = list(range(0, self.pairs, 2)) + list(range(1, self.pairs, 2))[::-1]
        self.device = [[2 * c, 2 * c + 1] for c in chips]
        self.place = {self.device[i][k]: (i, k) for i in range(self.pairs) for k in (0, 1)}

    def at(self, i, k):
        return self.device[i % self.pairs][k]

    def way(self, g, k):
        return 1 if (g + k) % 2 == 0 else -1

    def step(self):
        return [
            (g * self.count + e, g * self.count + self.at(i + self.way(g, k), k))
            for g in range(self.groups)
            for e, (i, k) in self.place.items()
        ]

    def back(self, flip_lane):
        return [
            (g * self.count + self.at(i + self.way(g, k), k ^ flip_lane), g * self.count + e)
            for g in range(self.groups)
            for e, (i, k) in self.place.items()
        ]

    def sibling(self):
        return [(e, e ^ 1) for e in range(self.count)]

    def source(self, place, s, flip_lane):
        me, odd = lax.rem(place, self.count), place // self.count
        chip, lane = me // 2, lax.rem(me, 2)
        evens = (self.pairs + 1) // 2
        i = jnp.where(lax.rem(chip, 2) == 0, chip // 2, self.pairs - 1 - chip // 2)
        way = 1 - 2 * lax.rem(odd + lane, 2)
        i = lax.rem(i - s * way + 2 * self.pairs, self.pairs)
        chip = jnp.where(i < evens, 2 * i, 2 * (self.pairs - 1 - i) + 1)
        return 2 * chip + lax.rem(lane + flip_lane, 2)


def swap_pairs(axis):
    count = lax.axis_size(axis)
    route = []
    for low in range(0, count - 1, 2):
        route += [(low, low + 1), (low + 1, low)]
    return route


def attend_body(first, count, after, len_ref, q_ref, kv_ref, cache_ref, far_ref, *refs):
    out_ref = refs[after]
    rows = q_ref.shape[0]
    seg = far_ref.shape[1]
    dims = (((1,), (1,)), ((), ()))
    unit = (lax.broadcasted_iota(jnp.int32, (rows, HD), 1) == 0).astype(BF16)
    mark = lax.dot_general(unit, far_ref[0, :, :HD], dims, preferred_element_type=F32)
    near_ok = lax.broadcasted_iota(jnp.int32, (rows, seg), 1) < len_ref[0, 0]
    far_ok = mark < DEAD / 2
    scale = 1.0 / math.sqrt(HD)
    for h in range(count):
        cols = slice((first + h) * HD, (first + h + 1) * HD)
        own = slice(h * HD, (h + 1) * HD)
        q = q_ref[:, cols]
        s0 = lax.dot_general(q, kv_ref[0, :, cols], dims, preferred_element_type=F32) * scale
        s1 = lax.dot_general(q, cache_ref[0, 0, 0, :, cols], dims, preferred_element_type=F32) * scale
        s2 = lax.dot_general(q, far_ref[0, :, own], dims, preferred_element_type=F32) * scale
        s1 = jnp.where(near_ok, s1, -1e30)
        s2 = jnp.where(far_ok, s2, -1e30)
        m = jnp.max(jnp.maximum(jnp.maximum(s0, s1), s2), axis=1, keepdims=True)
        w0 = jnp.exp(s0 - m)
        w1 = jnp.where(near_ok, jnp.exp(s1 - m), 0.0)
        w2 = jnp.where(far_ok, jnp.exp(s2 - m), 0.0)
        l = jnp.sum(w0 + w1 + w2, axis=1, keepdims=True)
        a = jnp.dot(w0.astype(BF16), kv_ref[1, :, cols], preferred_element_type=F32)
        a += jnp.dot(w1.astype(BF16), cache_ref[1, 0, 0, :, cols], preferred_element_type=F32)
        a += jnp.dot(w2.astype(BF16), far_ref[1, :, own], preferred_element_type=F32)
        out_ref[h] = (a / l).astype(BF16)


def far_body(len_ref, cache_ref, out_ref, sems):
    copies = [pltpu.make_async_copy(cache_ref.at[i, 0, 1], out_ref.at[i], sems.at[i]) for i in (0, 1)]
    for copy in copies:
        copy.start()
    for copy in copies:
        copy.wait()
    row = lax.broadcasted_iota(jnp.int32, out_ref.shape[1:], 0)
    out_ref[0] = jnp.where(row < len_ref[0, 1], out_ref[0].astype(F32), DEAD).astype(BF16)


def far_segment(seg_len, cache_kv):
    return pl.pallas_call(
        far_body,
        out_shape=jax.ShapeDtypeStruct((2,) + cache_kv.shape[3:], BF16),
        in_specs=[scalars(), in_hbm()],
        out_specs=full(),
        scratch_shapes=[pltpu.SemaphoreType.DMA((2,))],
        cost_estimate=cost(1.7),
        compiler_params=pltpu.CompilerParams(vmem_limit_bytes=FAR_MIB * 2**20),
        name="far_segment",
    )(seg_len, cache_kv)


def cost(micros):
    return pl.CostEstimate(flops=int(micros * 1e9 * SPEED), bytes_accessed=1000, transcendentals=0)


def full():
    return pl.BlockSpec(memory_space=pltpu.VMEM)


def scalars():
    return pl.BlockSpec(memory_space=SMEM)


def in_hbm():
    return pl.BlockSpec(memory_space=pltpu.HBM)


def anywhere():
    return pl.BlockSpec(memory_space=pl.ANY)


def attend(first, count, queries, span_kv, cache_kv, far, seg_len, held=None, after=()):
    rows = queries.shape[0]
    out = [jax.ShapeDtypeStruct((count, rows, HD), BF16)]
    passed = [] if held is None else [held]
    out += [jax.ShapeDtypeStruct(p.shape, p.dtype) for p in passed]
    return pl.pallas_call(
        functools.partial(attend_body, first, count, len(passed) + len(after)),
        out_shape=out,
        grid=(1,),
        in_specs=[scalars()]
        + [full()] * 3
        + [pl.BlockSpec((2, far.shape[1], count * HD), lambda i: (0, 0, first // count))]
        + [anywhere()] * (len(passed) + len(after)),
        out_specs=[full()] + [anywhere()] * len(passed),
        input_output_aliases={5: 1} if passed else {},
        cost_estimate=cost(2.4),
        compiler_params=pltpu.CompilerParams(vmem_limit_bytes=ATT_MIB * 2**20),
        name="attend",
    )(seg_len, queries, span_kv, cache_kv, far, *passed, *after)


def pack_body(count, lane_ref, rows_ref, routes_ref, wts_ref, own_ref, other_ref, tail_ref):
    slab, half = rows_ref.shape[0], own_ref.shape[1]
    lane = lane_ref[0]
    own_ref[:slab] = rows_ref[:, pl.ds(pl.multiple_of(lane * half, HD), half)]
    other_ref[:slab] = rows_ref[:, pl.ds(pl.multiple_of((1 - lane) * half, HD), half)]
    routes = routes_ref[...]
    wts = wts_ref[...]
    tokens = wts.shape[1]
    high, low = [], []
    for group in range(count // 8):
        dense = jnp.concatenate(
            [
                jnp.sum(jnp.where(routes == group * 8 + j, wts, 0.0), axis=0, keepdims=True)
                for j in range(8)
            ],
            axis=0,
        )
        top = dense.astype(BF16)
        high.append(top)
        low.append((dense - top.astype(F32)).astype(BF16))
    tail = jnp.concatenate(high + low, axis=1)
    for out in (own_ref, other_ref):
        out[slab:, : tail.shape[1]] = tail
        if tail.shape[1] < half:
            out[slab:, tail.shape[1] :] = jnp.zeros((8, half - tail.shape[1]), BF16)
    tail_ref[:8, : tail.shape[1]] = tail
    tail_ref[8:, : tail.shape[1]] = jnp.zeros_like(tail)
    if tail.shape[1] < half:
        tail_ref[:, tail.shape[1] :] = jnp.zeros((16, half - tail.shape[1]), BF16)


def pack(count, lane, o_rows, routes, route_wts):
    slab, width = o_rows.shape
    out = jax.ShapeDtypeStruct((slab + 8, width // 2), BF16)
    return pl.pallas_call(
        functools.partial(pack_body, count),
        out_shape=(out, out, jax.ShapeDtypeStruct((16, width // 2), BF16)),
        in_specs=[scalars()] + [full()] * 3,
        out_specs=(full(), full(), full()),
        cost_estimate=cost(0.7),
        compiler_params=pltpu.CompilerParams(vmem_limit_bytes=8 * 2**20),
        name="pack",
    )(lane, o_rows, routes.T, route_wts.T)


def project_body(ring, steps, blocks, pieces, carried, here, tail, me_ref, *refs):
    refs = list(refs)
    mine = [refs.pop(0) for _ in range(pieces)]
    theirs = [refs.pop(0) for _ in range(pieces)]
    before = [refs.pop(0) for _ in range(2 if carried else 0)]
    source = [refs.pop(0) for _ in range(blocks)]
    tail_refs = [refs.pop(0) for _ in range(tail)]
    own_ref, give_ref, wts_ref, att = refs[:4]
    rows = own_ref.shape[0]
    slab = att.shape[2]
    count = att.shape[0]
    copies = []
    if here < blocks:
        held, sems = refs[4:]
        away = range(blocks - here)
        copies = [pltpu.make_async_copy(source[b], held.at[b], sems.at[b]) for b in away]
        for copy in copies:
            copy.start()
        source = [held.at[b] for b in away] + source[blocks - here :]
    at = 0
    for a, b in zip(mine, theirs):
        att[at : at + a.shape[0], :rows] = a[...]
        att[at : at + a.shape[0], rows:] = b[...]
        at += a.shape[0]
    place = me_ref[0]
    me = lax.rem(place, count)
    sub, group = lax.rem(me, 8), me // 8
    groups = count // 8
    pick = lax.broadcasted_iota(jnp.int32, (8, rows), 0) == sub

    def line(ref, at):
        high = ref[at : at + 8, pl.ds(pl.multiple_of(group * rows, 128), rows)].astype(F32)
        low = ref[at : at + 8, pl.ds(pl.multiple_of((groups + group) * rows, 128), rows)].astype(F32)
        return jnp.sum(jnp.where(pick, high + low, 0.0), axis=0, keepdims=True)

    total = None
    lines = [None] * blocks
    for b in [*range(blocks - here, blocks), *range(blocks - here)]:
        if b < len(copies):
            copies[b].wait()
        head = att[ring.source(place, steps[b // 2], b % 2)]
        part = jnp.dot(head, source[b][:slab], preferred_element_type=F32)
        total = part if total is None else total + part
        if b >= tail:
            lines[b] = line(source[b], slab)
    for i, ref in enumerate(tail_refs):
        lines[i] = line(ref, 0)
    if carried:
        own_ref[...] = before[0][...] + total[:rows]
        give_ref[...] = (before[1][...] + total[rows:]).astype(give_ref.dtype)
    else:
        own_ref[...] = total[:rows]
        give_ref[...] = total[rows:]
    lines.append(jnp.zeros((128 - blocks, rows), F32))
    wts_ref[...] = jnp.concatenate(lines, axis=0).T


def project(ring, place, steps, mine, theirs, before, blocks, here, tails=()):
    count = sum(part.shape[0] for part in mine)
    rows, slab = mine[0].shape[1:]
    half = blocks[0].shape[1]
    out = jax.ShapeDtypeStruct((rows, half), F32)
    number = len(blocks)
    scratch = [pltpu.VMEM((count, 2 * rows, slab), BF16)]
    away = number - here
    if away:
        scratch += [pltpu.VMEM((away,) + blocks[0].shape, BF16), pltpu.SemaphoreType.DMA((away,))]
    return pl.pallas_call(
        functools.partial(
            project_body, ring, steps, number, len(mine), bool(before), here, len(tails)
        ),
        out_shape=(
            out,
            jax.ShapeDtypeStruct((rows, half), BF16 if before else F32),
            jax.ShapeDtypeStruct((rows, 128), F32),
        ),
        in_specs=[scalars()]
        + [full()] * (2 * len(mine) + len(before))
        + [in_hbm()] * away
        + [full()] * here
        + [full()] * len(tails),
        out_specs=(full(), full(), full()),
        scratch_shapes=scratch,
        cost_estimate=pl.CostEstimate(
            flops=4 * rows * half * slab * number, bytes_accessed=2 * half * slab * number, transcendentals=0
        ),
        compiler_params=pltpu.CompilerParams(vmem_limit_bytes=PRO_MIB * 2**20),
        name="project",
    )(place, *mine, *theirs, *before, *blocks, *tails)


def norm_body(lane_ref, resid_ref, own_ref, got_ref, gain_ref, sum_ref, out_ref):
    first = lane_ref[0] == 0
    half = own_ref.shape[1]
    own = own_ref[...]
    got = got_ref[...].astype(F32)
    low = resid_ref[:, :half].astype(F32) + jnp.where(first, own, got)
    high = resid_ref[:, half:].astype(F32) + jnp.where(first, got, own)
    sum_ref[:, :half] = low
    sum_ref[:, half:] = high
    square = jnp.sum(low * low + high * high, axis=1, keepdims=True)
    scale = lax.rsqrt(square * (1.0 / (2 * half)) + 1e-05)
    out_ref[:, :half] = (low * scale * gain_ref[:, :half]).astype(BF16)
    out_ref[:, half:] = (high * scale * gain_ref[:, half:]).astype(BF16)


def norm(lane, resid, own, got, gain):
    return pl.pallas_call(
        norm_body,
        out_shape=(
            jax.ShapeDtypeStruct(resid.shape, F32),
            jax.ShapeDtypeStruct(resid.shape, BF16),
        ),
        in_specs=[scalars()] + [full()] * 4,
        out_specs=(full(), full()),
        cost_estimate=cost(0.4),
        compiler_params=pltpu.CompilerParams(vmem_limit_bytes=16 * 2**20),
        name="norm",
    )(lane, resid, own, got, gain.reshape(1, -1))


def expert_body(cols, parts, after, gives, *refs):
    refs = list(refs)
    xy, (wx_ref, wy_ref, in_ref, down_ref) = refs[: 2 * parts], refs[2 * parts : 2 * parts + 4]
    cx_ref, *cy_refs = refs[2 * parts + 4 + after :]
    rows, width = cx_ref.shape
    size = rows // gives
    both = jnp.concatenate([ref[...] for ref in xy], axis=0)
    gate = jnp.dot(both, in_ref[0, :, :FF], preferred_element_type=F32)
    up = jnp.dot(both, in_ref[0, :, FF:], preferred_element_type=F32)
    hidden = (gate * jax.nn.sigmoid(gate) * up).astype(BF16)
    wx = wx_ref[:, cols[0] : cols[0] + 1]
    wy = wy_ref[:, cols[1] : cols[1] + 1]
    step = 512
    for at in range(0, width, step):
        out = jnp.dot(hidden, down_ref[0, :, at : at + step], preferred_element_type=F32)
        cx_ref[:, at : at + step] = (out[:rows] * wx).astype(BF16)
        cy = (out[rows:] * wy).astype(BF16)
        for i, cy_ref in enumerate(cy_refs):
            cy_ref[:, at : at + step] = cy[i * size : (i + 1) * size]


def expert(cols, x, y, wx, wy, w_in, w_out, after=(), gives=1):
    rows, width = wx.shape[0], w_out.shape[2]
    parts = len(x)
    out = jax.ShapeDtypeStruct((rows, width), BF16)
    part = jax.ShapeDtypeStruct((rows // gives, width), BF16)
    return pl.pallas_call(
        functools.partial(expert_body, cols, parts, len(after), gives),
        out_shape=(out,) + (part,) * gives,
        in_specs=[full()] * (2 * parts + 4) + [anywhere()] * len(after),
        out_specs=(full(),) * (1 + gives),
        cost_estimate=cost(EXPERT_COST),
        compiler_params=pltpu.CompilerParams(vmem_limit_bytes=EXP_MIB * 2**20),
        name="expert",
    )(*x, *y, wx, wy, w_in, w_out, *after)


def add_body(cuts, *refs):
    total = None
    at = 0
    for cut in cuts:
        term = jnp.concatenate([ref[c].astype(F32) for ref, c in zip(refs[at:], cut)], axis=0)
        at += len(cut)
        total = term if total is None else total + term
    refs[-1][...] = total.astype(refs[-1].dtype)


def add(cut, rows, terms, kind):
    used, cuts = [], []
    for term in terms:
        size = rows // len(term)
        mine = []
        for i, part in enumerate(term):
            low, high = max(cut.start - i * size, 0), min(cut.stop - i * size, size)
            if low < high:
                used.append(part)
                mine.append(slice(low, high))
        cuts.append(mine)
    return pl.pallas_call(
        functools.partial(add_body, cuts),
        out_shape=jax.ShapeDtypeStruct((cut.stop - cut.start, used[0].shape[1]), kind),
        in_specs=[full()] * len(used),
        out_specs=full(),
        cost_estimate=cost(ADD_COST),
        compiler_params=pltpu.CompilerParams(vmem_limit_bytes=8 * 2**20),
        name="add",
    )(*used)


def shards(
    ring, resid, queries, span_kv, cache_kv, seg_len, o_rows, norm_gain, routes, route_wts, w_in, w_out
):
    count, pairs = ring.count, ring.pairs
    rows, width = queries.shape
    me = lax.axis_index("expert")
    lane = me % 2
    forward, sibling = ring.step(), ring.sibling()
    place = lax.axis_index("group") % 2 * count + me

    def ahead(block, name="rows out"):
        with jax.named_scope(name):
            return lax.ppermute(block, ("group", "expert"), forward)

    def across(block, name="to sibling"):
        with jax.named_scope(name):
            return lax.ppermute(block, "expert", sibling)

    group_swap = swap_pairs("group")
    groups = 4
    heads = HEADS // groups
    wide = heads * HD
    groups = 4
    heads = HEADS // groups
    slab = o_rows.shape[0]
    with jax.named_scope("far segment"):
        far = lax.ppermute(far_segment(seg_len, cache_kv), "group", group_swap)

    chain_a, other, tail = pack(count, lane[None], o_rows, routes, route_wts)
    chain_b = across(other)
    blocks = [chain_a, chain_b]
    mine, theirs = [], []
    chains = [chain_a, chain_b]
    last = []

    def heads_of(j, held=None, after=()):
        part, *held = attend(j * heads, heads, queries, span_kv, cache_kv, far, seg_len, held, after)
        mine.append(part)
        theirs.append(across(part, f"attended {j}"))
        return held

    for s in range(1, pairs - HOPS_X):
        chains = [ahead(part, f"o rows {s}{'ab'[i]}") for i, part in enumerate(chains)]
        if s <= HOPS_X:
            with jax.named_scope("o rows of partner"):
                last.append([lax.ppermute(part, "group", group_swap) for part in chains])
        if s == HELD:
            (chains[0],) = heads_of(0, chains[0])
        blocks += chains
    if HELD == 0:
        heads_of(0)
    for j in range(1, groups):
        heads_of(j, after=last[AFTER[j]] if j in AFTER and AFTER[j] < len(last) else ())
    order = list(range(pairs - 1 - HOPS_X)) + list(range(pairs - HOPS_X, pairs)) + [pairs - 1 - HOPS_X]
    blocks, ends = blocks[:-2], blocks[-2:]
    for pair in reversed(last):
        blocks += pair
    blocks += ends
    tails = []
    with jax.named_scope("gate weights back"):
        for route in (ring.back(0), ring.back(1)) if HOPS_X else ():
            tails.append(lax.ppermute(tail, ("group", "expert"), route))
    if slab != HD:
        mine, theirs = (
            [jnp.concatenate(p).transpose(1, 0, 2).reshape(rows, count, slab).transpose(1, 0, 2)]
            for p in (mine, theirs)
        )
    early = 2 * (pairs - 1 - HOPS_X)
    place = place[None]
    first_own, first_give, wts_early = project(ring, place, order[: early // 2], mine, theirs, [], blocks[:early], 0)
    own, give, wts_late = project(
        ring, place, order[early // 2 :], mine, theirs, [first_own, first_give], blocks[early:], 2, tails
    )
    got = across(give, "projected")
    residual, normed = norm(lane[None], resid, own, got, norm_gain)

    def gate_at(step, flip):
        column = 2 * order.index(step) + flip
        return (wts_early, column) if column < early else (wts_late, column - early)

    size = rows // AGP
    x = [[normed[p * size : (p + 1) * size] for p in range(AGP)]]
    y = [[across(part, "normed") for part in x[0]]]

    def sums(s, after=()):
        wx, column_x = gate_at(s, 0)
        wy, column_y = gate_at((pairs - s) % pairs, 1)
        keep, *give = expert((column_x, column_y), x[s], y[s], wx, wy, w_in, w_out, after, GIVE)
        return keep, [across(part, f"sums across {s}{'ab'[i]}") for i, part in enumerate(give)]

    def combine(terms, parts, kind=BF16):
        terms = [term if isinstance(term, list) else [term] for term in terms if len(term)]
        return [
            add(slice(p * rows // parts, (p + 1) * rows // parts), rows, terms, kind) for p in range(parts)
        ]

    travelling = []
    for s in range(1, pairs):
        x.append([ahead(part, f"rows out {s}{'ab'[i]}") for i, part in enumerate(x[-1])])
        y.append([across(part, f"rows across {s}{'ab'[i]}") for i, part in enumerate(x[-1])])
        keep, back = sums(s)
        total = combine([keep, back, travelling], 2 if s in HALVED else 1)
        travelling = [ahead(part, f"sums out {s}{'ab'[i]}") for i, part in enumerate(total)]
    base = combine([residual, *sums(0, (x[min(LATE, pairs - 1)][0],))], 1, F32)
    return combine([base, travelling], 1)[0]


def solution(mesh):
    placed = (
        P(("group", "expert"), None),
        P(("group", "expert"), None),
        P(None, ("group", "expert"), None),
        P(None, ("group", "expert"), None, None, None),
        P(("group", "expert"), None),
        P("expert", None),
        P(),
        P(("group", "expert"), None),
        P(("group", "expert"), None),
        P("expert", None, None),
        P("expert", None, None),
    )
    ring = Ring(mesh.shape["group"], mesh.shape["expert"])
    return jax.shard_map(
        functools.partial(shards, ring),
        mesh=mesh,
        in_specs=placed,
        out_specs=P(("group", "expert"), None),
        check_vma=False,
    )
```
